32 devices in a mesh: grp: 2 (over x), ctx: 16 (over z, y, core).
Axes of the slice: x: 2, y: 2, z: 4, core: 2. Of those that a mesh axis runs over, the one named last changes fastest.
Arguments:
- queries: bfloat16 [4, 4, 128, 576], P('grp', None, 'ctx'), parts along dimension 0, may hold values from -40 to 40
- latent_cache: bfloat16 [4, 32768, 576], P('grp', 'ctx'), parts along dimension 0, may hold values from -64 to 64
- lengths: int32 [4], P('grp'), parts along dimension 0, may hold values from 16384 to 32768
- draft_mask: int32 [4, 4], P('grp'), parts along dimension 0, may hold values 0 or 1
- value_up: bfloat16 [128, 512, 128], P('ctx'), may hold values from -0.8984375 to 0.8984375
- output_weight: bfloat16 [16384, 7168], P('ctx'), may hold values from -0.046875 to 0.046875
Outputs:
- reduced: bfloat16 [4, 4, 7168], P('grp', None, 'ctx'), parts along dimension 0
The draws below stay inside these ranges and needn't reach their ends.
There are 2 independent parts, one for each index of `grp`. The reference program is written for one: setup_inputs(seed, part) draws one part's arguments, and reference() takes and returns one part's arrays. A program takes and returns all parts, laid end to end along the dimension named above; an argument that names none is the same for every part. Nothing has to cross between parts.
Inputs may be any that keep to these rules, and one draw needn't show every extreme that they name: `lengths`: each request has at least 16384 cached positions, so every row sees some position.
All inputs are finite; a program needn't handle non-finite values.
Results may differ from the reference program's by a relative error of at most 0.015.
Values may be sent and summed in bfloat16 or wider, within the bound.
No kernel may reach another device: no remote copies, remote signals or barrier semaphores. Data moves between devices by JAX's collectives and lax.ppermute only.
A program may use at most 64 MiB of HBM per device.

```python
from functools import partial
import jax
import jax.numpy as jnp
from jax import lax

HEADS = 128
LATENT = 512
ROPE = 64
VHEAD = 128
DMODEL = 7168
REQS = 2
SPEC = 4
CTX_DEV = 2048
LEN = 32768
N_CTX = 16


def draw_latent_cache(key, part):
    own_key = jax.random.fold_in(key, 1)
    latent = jnp.clip(jax.random.normal(own_key, (REQS, LEN, LATENT + ROPE)), -6.0, 6.0)
    return latent.astype(jnp.bfloat16)


def draw_queries(key, part):
    own_key = jax.random.fold_in(key, 2)
    spread = 1.7320508
    query_all = jnp.clip(spread * jax.random.normal(own_key, (REQS, SPEC, HEADS, LATENT + ROPE)), -6.0 * spread, 6.0 * spread)
    return query_all.astype(jnp.bfloat16)


def touch_ends(values, stream_key, smallest, top_value):
    longest = values.shape.index(max(values.shape))
    spots = []
    for shift in (0, 1):
        where = [jax.random.randint(jax.random.fold_in(stream_key, axis), (), 0, length) for axis, length in enumerate(values.shape)]
        where[longest] = (where[longest] + shift) % values.shape[longest]
        spots.append(tuple(where))
    return values.at[spots[0]].set(smallest).at[spots[1]].set(top_value)


def level_of(rng, dims, cuts, low, high):
    loudness, own = 1.0, jax.random.fold_in(rng, 6)
    for axis_at, blocks in cuts:
        steps = jnp.exp(jax.random.uniform(jax.random.fold_in(own, axis_at), (blocks,), jnp.float32, low / len(cuts), high / len(cuts)))
        loudness = loudness * jnp.repeat(steps, dims[axis_at] // blocks).reshape([-1 if axis == axis_at else 1 for axis in range(len(dims))])
    return loudness


def normal_values(rng, dims, scale, limit, pieces=(), kind=jnp.bfloat16):
    values = scale * jax.random.normal(rng, dims, jnp.float32)
    if pieces:
        values = values * level_of(rng, dims, pieces, -0.22, 0.18)
    return jnp.clip(values, -limit, limit).astype(kind)


def setup_inputs(seed: int = 0, part: int = 0) -> dict:
    key_list = jax.random.split(jax.random.key(seed), 7)
    own_keys = jax.random.split(jax.random.fold_in(key_list[6], part), 7)
    return {
        "queries": draw_queries(jax.random.fold_in(jax.random.fold_in(key_list[6], part), 71), part),
        "latent_cache": draw_latent_cache(jax.random.fold_in(jax.random.fold_in(key_list[6], part), 71), part),
        "lengths": jax.random.randint(own_keys[2], (REQS,), LEN // 2, LEN + 1).astype(jnp.int32),
        "draft_mask": touch_ends((jax.random.randint(own_keys[3], (REQS, SPEC), 0, 4) < 3).astype(jnp.int32), jax.random.fold_in(own_keys[3], 1), 0, 1),
        "value_up": normal_values(key_list[4], (HEADS, LATENT, VHEAD), 0.15, 0.8984375, ((0, 16),)),
        "output_weight": normal_values(key_list[5], (HEADS * VHEAD, DMODEL), (HEADS * VHEAD) ** -0.5, 0.046875, ((0, 16),)),
    }


SOFTMAX_SCALE = 192.0 ** -0.5
SCORE_FLOOR = -1.0e30


def shard_terms(queries_wide, lengths, shard_item):
    key_block, offset = shard_item
    block_wide = key_block.astype(jnp.float32)
    scores = jnp.einsum("rshw,rcw->rshc", queries_wide, block_wide) * SOFTMAX_SCALE
    position = offset + jnp.arange(key_block.shape[1], dtype=jnp.int32)
    horizon = lengths[:, None] - SPEC + 1 + jnp.arange(SPEC, dtype=jnp.int32)[None, :]
    visible = (position[None, None, :] < horizon[:, :, None])[:, :, None, :]
    peak = jnp.max(jnp.where(visible, scores, SCORE_FLOOR), axis=-1)
    weights = jnp.where(visible, jnp.exp(scores - peak[..., None]), 0.0)
    denominator = jnp.sum(weights, axis=-1)
    weights_low = lax.optimization_barrier(weights.astype(jnp.bfloat16)).astype(jnp.float32)
    numerator = jnp.einsum("rshc,rcl->rshl", weights_low, block_wide[:, :, :LATENT])
    return peak, denominator, numerator


def reference(queries, latent_cache, lengths, draft_mask, value_up, output_weight):
    queries_wide = queries.astype(jnp.float32)
    blocks = jnp.swapaxes(latent_cache.reshape(REQS, N_CTX, CTX_DEV, LATENT + ROPE), 0, 1)
    starts = jnp.arange(N_CTX, dtype=jnp.int32) * CTX_DEV
    peak, denominator, numerator = lax.map(partial(shard_terms, queries_wide, lengths), (blocks, starts))
    largest = jnp.max(peak, axis=0)
    factor = jnp.exp(peak - largest)
    upper = jnp.sum(factor[..., None] * numerator, axis=0)
    lower = jnp.sum(factor * denominator, axis=0)
    attended = (upper / lower[..., None]).astype(jnp.bfloat16)
    values = jnp.einsum("rshc,hcd->rshd", attended.astype(jnp.float32), value_up.astype(jnp.float32)).astype(jnp.bfloat16)
    stacked = values.reshape(REQS * SPEC, HEADS * VHEAD)
    reduced = jnp.dot(stacked, output_weight, preferred_element_type=jnp.float32).reshape(REQS, SPEC, DMODEL)
    return (reduced * draft_mask[..., None].astype(jnp.float32)).astype(jnp.bfloat16)
```

```python
import functools
import math

import jax
import jax.numpy as jnp
from jax import lax
from jax.experimental import pallas as pl
from jax.experimental.pallas import tpu as pltpu
from jax.sharding import PartitionSpec as P

SOFTMAX_SCALE = 192.0 ** (-0.5)
LOG2_SCALE = SOFTMAX_SCALE * math.log2(math.e)
SCORE_FLOOR = -1e30
STAT_LANES = 128
MIB = 1024 * 1024


def split_low(x):
    high = x.astype(jnp.bfloat16).astype(jnp.float32)
    return high, (x - high).astype(jnp.bfloat16).astype(jnp.float32)


def attend_kernel(
    chunks, spec, heads, latent, width, lengths_ref, *refs
):
    q_refs = refs[:chunks]
    own_ref, got_ref = refs[chunks : chunks + 2]
    out_refs = refs[chunks + 2 : 2 * chunks + 2]
    keys, scores, sems = refs[2 * chunks + 2 :]
    me = lax.axis_index("ctx")
    core = lax.rem(me, 2)
    block = own_ref.shape[2]
    per_block = block // width
    steps = 2 * per_block
    copies = []
    for step in range(steps):
        source = own_ref if step < per_block else got_ref
        start = (step % per_block) * width
        copy = pltpu.make_async_copy(
            source.at[core, :, pl.ds(start, width)], keys.at[step], sems.at[step]
        )
        copy.start()
        copies.append(copy)
    queries = jnp.concatenate([ref[...] for ref in q_refs], axis=0)
    rows = queries.shape[0]
    row = lax.broadcasted_iota(jnp.int32, (rows, 1), 0)
    draft = lax.rem(lax.div(row, heads), spec)
    horizon = lengths_ref[core] - spec + 1 + draft
    bases = (me * block, (me + 1 - 2 * core) * block)
    peak = jnp.full((rows, 1), SCORE_FLOOR, jnp.float32)
    for step in range(steps):
        copies[step].wait()
        tile = jnp.dot(queries, keys[step], preferred_element_type=jnp.float32)
        start = bases[step // per_block] + (step % per_block) * width
        position = start + lax.broadcasted_iota(jnp.int32, (1, width), 1)
        tile = jnp.where(position < horizon, tile * LOG2_SCALE, SCORE_FLOOR)
        scores[step] = tile
        peak = jnp.maximum(peak, jnp.max(tile, axis=1, keepdims=True))
    peak_high, peak_low = split_low(jnp.maximum(peak, 0.1 * SCORE_FLOOR))
    peak = peak_high + peak_low
    denominator = jnp.zeros((rows, 1), jnp.float32)
    numerator = jnp.zeros((rows, latent), jnp.float32)
    for step in range(steps):
        weights = jnp.exp2(scores[step] - peak)
        denominator += jnp.sum(weights, axis=1, keepdims=True)
        numerator += lax.dot_general(
            weights.astype(jnp.bfloat16),
            keys[step, :latent],
            (((1,), (1,)), ((), ())),
            preferred_element_type=jnp.float32,
        )
    denom_high, denom_low = split_low(denominator)
    lane = lax.broadcasted_iota(jnp.int32, (rows, STAT_LANES), 1)
    stats = jnp.where(lane == 0, peak_high, jnp.where(lane == 1, peak_low, 0.0))
    stats = jnp.where(lane == 2, denom_high, jnp.where(lane == 3, denom_low, stats))
    chunk = rows // chunks
    for i, out_ref in enumerate(out_refs):
        part = slice(i * chunk, (i + 1) * chunk)
        out_ref[:, :latent] = numerator[part].astype(jnp.bfloat16)
        out_ref[:, latent:] = stats[part].astype(jnp.bfloat16)


def attend(lengths, query_chunks, own_keys, got_keys, spec, heads, latent):
    chunks = len(query_chunks)
    chunk, feature = query_chunks[0].shape
    block = own_keys.shape[2]
    width = min(block, 1024)
    steps = 2 * (block // width)
    rows = chunks * chunk
    flops = 2 * rows * 2 * block * (feature + latent)
    return pl.pallas_call(
        functools.partial(attend_kernel, chunks, spec, heads, latent, width),
        out_shape=[jax.ShapeDtypeStruct((chunk, latent + STAT_LANES), jnp.bfloat16)] * chunks,
        in_specs=[pl.BlockSpec(memory_space=pltpu.SMEM)]
        + [pl.BlockSpec(memory_space=pltpu.VMEM)] * chunks
        + [pl.BlockSpec(memory_space=pl.ANY)] * 2,
        out_specs=[pl.BlockSpec(memory_space=pltpu.VMEM)] * chunks,
        scratch_shapes=[
            pltpu.VMEM((steps, feature, width), jnp.bfloat16),
            pltpu.VMEM((steps, rows, width), jnp.float32),
            pltpu.SemaphoreType.DMA((steps,)),
        ],
        compiler_params=pltpu.CompilerParams(vmem_limit_bytes=32 * MIB),
        cost_estimate=pl.CostEstimate(
            flops=flops, bytes_accessed=4 * block * feature, transcendentals=rows * 2 * block
        ),
        name="attend",
    )(lengths, *query_chunks, own_keys, got_keys)


def merge_kernel(parts, latent, *refs):
    in_refs, (own_ref, give_ref) = refs[:parts], refs[parts:]
    peaks, denominators = [], []
    for ref in in_refs:
        stats = ref[:, latent:].astype(jnp.float32)
        peaks.append(stats[:, 0:1] + stats[:, 1:2])
        denominators.append(stats[:, 2:3] + stats[:, 3:4])
    largest = functools.reduce(jnp.maximum, peaks)
    upper, lower = 0.0, 0.0
    for ref, peak, denominator in zip(in_refs, peaks, denominators):
        factor = jnp.exp2(peak - largest)
        upper += factor * ref[:, :latent].astype(jnp.float32)
        lower += factor * denominator
    attended = (upper / lower).astype(jnp.bfloat16)
    half = attended.shape[0] // 2
    own_ref[...] = attended[:half]
    give_ref[...] = attended[half:]


def merge(parts, latent):
    rows = parts[0].shape[0]
    return pl.pallas_call(
        functools.partial(merge_kernel, len(parts), latent),
        out_shape=[jax.ShapeDtypeStruct((rows // 2, latent), jnp.bfloat16)] * 2,
        compiler_params=pltpu.CompilerParams(vmem_limit_bytes=16 * MIB),
        name="merge",
    )(*parts)


def project_kernel(spec, heads, owners, own_ref, got_ref, up_ref, weight_ref, out_ref, values_ref):
    step = pl.program_id(0)

    @pl.when(step == 0)
    def _():
        core = lax.rem(lax.axis_index("ctx"), 2)
        own, got = own_ref[...], got_ref[...]
        first = jnp.where(core == 0, own, got)
        second = jnp.where(core == 0, got, own)
        attended = jnp.concatenate([first, second], axis=0)
        rows = attended.shape[0]
        row = lax.broadcasted_iota(jnp.int32, (rows, 1), 0)
        head = lax.rem(row, heads)
        for h in range(heads):
            tile = jnp.dot(attended, up_ref[h], preferred_element_type=jnp.float32)
            tile = jnp.where(head == h, tile, 0.0)
            tile = jnp.sum(tile.reshape(rows // heads, heads, tile.shape[1]), axis=1)
            wide = tile.shape[1]
            values_ref[:, h * wide : (h + 1) * wide] = tile.astype(jnp.bfloat16)

    tile = jnp.dot(values_ref[...], weight_ref[...], preferred_element_type=jnp.float32)
    columns = out_ref.shape[2]
    for i in range(out_ref.shape[0]):
        out_ref[i] = tile[:, i * columns : (i + 1) * columns].astype(out_ref.dtype)


def project(own, got, value_up, weight, spec, owners):
    heads, latent, wide = value_up.shape
    depth, model = weight.shape
    columns = model // owners
    rows = 2 * spec
    group = next(g for g in (2, 1, 4, 8, 16, owners) if (g * columns) % 128 == 0)
    steps = owners // group
    return pl.pallas_call(
        functools.partial(project_kernel, spec, heads, owners),
        grid=(steps,),
        out_shape=jax.ShapeDtypeStruct((owners, rows, columns), jnp.bfloat16),
        in_specs=[
            pl.BlockSpec(own.shape, lambda i: (0, 0)),
            pl.BlockSpec(got.shape, lambda i: (0, 0)),
            pl.BlockSpec(value_up.shape, lambda i: (0, 0, 0)),
            pl.BlockSpec((depth, group * columns), lambda i: (0, i)),
        ],
        out_specs=pl.BlockSpec((group, rows, columns), lambda i: (i, 0, 0)),
        scratch_shapes=[pltpu.VMEM((rows, depth), jnp.bfloat16)],
        compiler_params=pltpu.CompilerParams(vmem_limit_bytes=24 * MIB),
        name="project",
    )(own, got, value_up, weight)


def finish_kernel(in_ref, mask_ref, out_ref):
    total = jnp.sum(in_ref[...].astype(jnp.float32), axis=0)
    spec = out_ref.shape[1]
    for r in range(out_ref.shape[0]):
        for j in range(spec):
            row = total[r * spec + j : r * spec + j + 1, :]
            kept = row * mask_ref[r, j].astype(jnp.float32)
            out_ref[r, j : j + 1, :] = kept.astype(out_ref.dtype)


def finish(parts, draft_mask):
    owners, rows, columns = parts.shape
    requests, spec = draft_mask.shape
    return pl.pallas_call(
        finish_kernel,
        out_shape=jax.ShapeDtypeStruct((requests, spec, columns), jnp.bfloat16),
        in_specs=[
            pl.BlockSpec(memory_space=pltpu.VMEM),
            pl.BlockSpec(memory_space=pltpu.SMEM),
        ],
        out_specs=pl.BlockSpec(memory_space=pltpu.VMEM),
        compiler_params=pltpu.CompilerParams(vmem_limit_bytes=16 * MIB),
        name="finish",
    )(parts, draft_mask)


def on_device(n, queries, latent_cache, lengths, draft_mask, value_up, output_weight):
    requests, spec, heads, feature = queries.shape
    latent = value_up.shape[1]
    core = lax.rem(lax.axis_index("ctx"), 2)

    def swap(x, bits):
        return lax.ppermute(x, "ctx", [(i, i ^ bits) for i in range(n)])

    chunk = requests * spec * heads
    got = swap(queries, 1)
    both = jnp.stack([queries, got], axis=1)
    mine = lax.dynamic_index_in_dim(both, core, 0, keepdims=False).reshape(chunk, feature)
    own_keys = jnp.swapaxes(latent_cache, 1, 2)
    got_keys = swap(own_keys, 1)

    peers = [2 * k for k in range(1, n // 2)]
    near = peers[: n // 4 - 1]
    far = peers[n // 4 - 1 :]
    far_queries = [swap(mine, bits) for bits in far]
    near_queries = [mine] + [swap(mine, bits) for bits in near]
    shared = (spec, heads, latent)
    near_parts = attend(lengths, near_queries, own_keys, got_keys, *shared)
    far_parts = attend(lengths, far_queries, own_keys, got_keys, *shared)
    parts = [near_parts[0]]
    parts += [swap(part, bits) for part, bits in zip(near_parts[1:], near)]
    parts += [swap(part, bits) for part, bits in zip(far_parts, far)]
    own, give = merge(parts, latent)
    outs = project(own, swap(give, 1), value_up, output_weight, spec, n)
    received = lax.all_to_all(outs, "ctx", 0, 0, tiled=True)
    return finish(received, draft_mask)


def solution(mesh):
    return jax.shard_map(
        functools.partial(on_device, mesh.shape["ctx"]),
        mesh=mesh,
        in_specs=(
            P("grp", None, "ctx", None),
            P("grp", "ctx", None),
            P("grp"),
            P("grp", None),
            P("ctx", None, None),
            P("ctx", None),
        ),
        out_specs=P("grp", None, "ctx"),
        check_vma=False,
    )
```

```python
import functools
import math

import jax
import jax.numpy as jnp
from jax import lax
from jax.experimental import pallas as pl
from jax.experimental.pallas import tpu as pltpu
from jax.sharding import PartitionSpec as P

SOFTMAX_SCALE = 192.0 ** (-0.5)
LOG2_SCALE = SOFTMAX_SCALE * math.log2(math.e)
SCORE_FLOOR = -1e30
STAT_LANES = 128
MIB = 1024 * 1024


def split_low(x):
    high = x.astype(jnp.bfloat16).astype(jnp.float32)
    return high, (x - high).astype(jnp.bfloat16).astype(jnp.float32)


def attend_kernel(chunks, spec, heads, latent, lengths_ref, *refs):
    q_refs, key_refs, out_refs = refs[:chunks], refs[chunks : chunks + 2], refs[chunks + 2 :]
    block = key_refs[0].shape[1]
    width = min(block, 512)
    per_block = block // width
    steps = 2 * per_block
    me = lax.axis_index("ctx")
    bases = (me * block, (me + 1 - 2 * lax.rem(me, 2)) * block)
    queries = jnp.concatenate([ref[...] for ref in q_refs], axis=0)
    rows = queries.shape[0]
    row = lax.broadcasted_iota(jnp.int32, (rows, 1), 0)
    draft = lax.rem(lax.div(row, heads), spec)
    horizon = lengths_ref[pl.ds(lax.rem(me, 2), 1), :1] - spec + 1 + draft

    def keys(step, features):
        start = (step % per_block) * width
        return key_refs[step // per_block][:features, start : start + width]

    def score(step):
        tile = jnp.dot(queries, keys(step, None), preferred_element_type=jnp.float32)
        start = bases[step // per_block] + (step % per_block) * width
        position = start + lax.broadcasted_iota(jnp.int32, (1, width), 1)
        return jnp.where(position < horizon, tile * LOG2_SCALE, SCORE_FLOOR)

    peak = jnp.full((rows, 1), 0.1 * SCORE_FLOOR, jnp.float32)
    denominator = jnp.zeros((rows, 1), jnp.float32)
    numerator = jnp.zeros((rows, latent), jnp.float32)
    tile = score(0)
    for step in range(steps):
        following = score(step + 1) if step + 1 < steps else None
        higher = jnp.maximum(peak, jnp.max(tile, axis=1, keepdims=True))
        if step == steps - 1:
            higher = sum(split_low(higher))
        weights = jnp.exp2(tile - higher)
        ratio = jnp.exp2(peak - higher)
        denominator = denominator * ratio + jnp.sum(weights, axis=1, keepdims=True)
        numerator = numerator * ratio + lax.dot_general(
            weights.astype(jnp.bfloat16),
            keys(step, latent),
            (((1,), (1,)), ((), ())),
            preferred_element_type=jnp.float32,
        )
        peak, tile = higher, following
    chunk = rows // chunks
    for i, out_ref in enumerate(out_refs):
        part = slice(i * chunk, (i + 1) * chunk)
        store_part(out_ref, latent, peak[part], denominator[part], numerator[part])


def attend(lengths, query_chunks, keys, spec, heads, latent):
    chunks = len(query_chunks)
    chunk, feature = query_chunks[0].shape
    rows, positions = chunks * chunk, 2 * keys[0].shape[1]
    return pl.pallas_call(
        functools.partial(attend_kernel, chunks, spec, heads, latent),
        out_shape=[jax.ShapeDtypeStruct((chunk, latent + STAT_LANES), jnp.bfloat16)] * chunks,
        compiler_params=pltpu.CompilerParams(vmem_limit_bytes=12 * MIB),
        cost_estimate=pl.CostEstimate(
            flops=2 * rows * positions * (feature + latent),
            bytes_accessed=2 * positions * feature,
            transcendentals=rows * positions,
        ),
        name="attend",
    )(lengths, *query_chunks, *keys)


def merged(in_refs, latent):
    peaks, denominators = [], []
    for ref in in_refs:
        stats = ref[:, latent:].astype(jnp.float32)
        peaks.append(stats[:, 0:1] + stats[:, 1:2])
        denominators.append(stats[:, 2:3] + stats[:, 3:4])
    largest = functools.reduce(jnp.maximum, peaks)
    upper, lower = 0.0, 0.0
    for ref, peak, denominator in zip(in_refs, peaks, denominators):
        factor = jnp.exp2(peak - largest)
        upper += factor * ref[:, :latent].astype(jnp.float32)
        lower += factor * denominator
    return largest, lower, upper


def store_part(ref, latent, peak, denominator, numerator):
    peak_high, peak_low = split_low(peak)
    denom_high, denom_low = split_low(denominator)
    lane = lax.broadcasted_iota(jnp.int32, (ref.shape[0], STAT_LANES), 1)
    stats = jnp.where(lane == 0, peak_high, jnp.where(lane == 1, peak_low, 0.0))
    stats = jnp.where(lane == 2, denom_high, jnp.where(lane == 3, denom_low, stats))
    ref[:, :latent] = numerator.astype(jnp.bfloat16)
    ref[:, latent:] = stats.astype(jnp.bfloat16)


def combine_kernel(parts, latent, *refs):
    store_part(refs[parts], latent, *merged(refs[:parts], latent))


def combine(parts, latent):
    return pl.pallas_call(
        functools.partial(combine_kernel, len(parts), latent),
        out_shape=jax.ShapeDtypeStruct(parts[0].shape, jnp.bfloat16),
        compiler_params=pltpu.CompilerParams(vmem_limit_bytes=8 * MIB),
        name="combine",
    )(*parts)


def merge_kernel(parts, latent, *refs):
    _, lower, upper = merged(refs[:parts], latent)
    own_ref, give_ref = refs[parts:]
    attended = (upper / lower).astype(jnp.bfloat16)
    half = attended.shape[0] // 2
    own_ref[...] = attended[:half]
    give_ref[...] = attended[half:]


def merge(parts, latent):
    rows = parts[0].shape[0]
    return pl.pallas_call(
        functools.partial(merge_kernel, len(parts), latent),
        out_shape=[jax.ShapeDtypeStruct((rows // 2, latent), jnp.bfloat16)] * 2,
        compiler_params=pltpu.CompilerParams(vmem_limit_bytes=8 * MIB),
        name="merge",
    )(*parts)


def project_kernel(heads, group, own_ref, got_ref, up_ref, weight_ref, out_ref):
    core = lax.rem(lax.axis_index("ctx"), 2)
    own, got = own_ref[...], got_ref[...]
    first = jnp.where(core == 0, own, got)
    second = jnp.where(core == 0, got, own)
    attended = jnp.concatenate([first, second], axis=0)
    rows = attended.shape[0]
    head = lax.rem(lax.broadcasted_iota(jnp.int32, (rows, 1), 0), heads)
    values = []
    for h in range(heads):
        tile = jnp.dot(attended, up_ref[h], preferred_element_type=jnp.float32)
        tile = jnp.where(head == h, tile, 0.0)
        tile = jnp.sum(tile.reshape(rows // heads, heads, tile.shape[1]), axis=1)
        values.append(tile.astype(jnp.bfloat16))
    values = jnp.concatenate(values, axis=1)
    owners, _, columns = out_ref.shape
    for i in range(0, owners, group):
        part = weight_ref[:, i * columns : (i + group) * columns]
        tile = jnp.dot(values, part, preferred_element_type=jnp.float32)
        for j in range(group):
            piece = tile[:, j * columns : (j + 1) * columns]
            out_ref[i + j] = piece.astype(out_ref.dtype)


def project(own, got, value_up, weight, spec, owners):
    heads = own.shape[0] // spec
    columns = weight.shape[1] // owners
    group = next(g for g in (2, 1, 4, 8, 16, owners) if (g * columns) % 128 == 0)
    return pl.pallas_call(
        functools.partial(project_kernel, heads, group),
        out_shape=jax.ShapeDtypeStruct((owners, 2 * spec, columns), jnp.bfloat16),
        in_specs=[pl.BlockSpec(memory_space=pltpu.VMEM)] * 4,
        out_specs=pl.BlockSpec(memory_space=pltpu.VMEM),
        compiler_params=pltpu.CompilerParams(vmem_limit_bytes=12 * MIB),
        name="project",
    )(own, got, value_up, weight)


def finish_kernel(in_ref, keep_ref, out_ref):
    total = jnp.sum(in_ref[...].astype(jnp.float32), axis=0) * keep_ref[:, :1]
    spec = out_ref.shape[1]
    for r in range(out_ref.shape[0]):
        out_ref[r] = total[r * spec : (r + 1) * spec].astype(out_ref.dtype)


def finish(parts, keep, requests):
    _, rows, columns = parts.shape
    return pl.pallas_call(
        finish_kernel,
        out_shape=jax.ShapeDtypeStruct((requests, rows // requests, columns), jnp.bfloat16),
        compiler_params=pltpu.CompilerParams(vmem_limit_bytes=8 * MIB),
        name="finish",
    )(parts, keep)


def on_device(n, queries, latent_cache, lengths, draft_mask, value_up, output_weight):
    requests, spec, heads, feature = queries.shape
    latent = value_up.shape[1]
    core = lax.rem(lax.axis_index("ctx"), 2)

    def swap(x, bits):
        return lax.ppermute(x, "ctx", [(i, i ^ bits) for i in range(n)])

    chunk = requests * spec * heads
    got = swap(queries, 1)
    both = jnp.stack([queries, got], axis=1)
    mine = lax.dynamic_index_in_dim(both, core, 0, keepdims=False).reshape(chunk, feature)
    own_keys = jnp.swapaxes(latent_cache, 1, 2)
    own_keys = lax.optimization_barrier((own_keys, got))[0]
    got_keys = swap(own_keys, 1)

    far_bit = n // 2
    near = [2 * k for k in range(1, n // 4)]
    far = swap(mine, far_bit)
    near_queries = [swap(mine, bits) for bits in near]

    own_keys, draft_mask = lax.optimization_barrier((own_keys, draft_mask, mine))[:2]
    keys = [lax.dynamic_index_in_dim(k, core, 0, keepdims=False) for k in (own_keys, got_keys)]
    far, keys, near_queries = lax.optimization_barrier((far, keys, near_queries))
    far_queries = [swap(far, bits) for bits in near]
    spread = jnp.broadcast_to(lengths[:, None], (requests, STAT_LANES))
    keep = draft_mask.astype(jnp.float32).reshape(requests * spec, 1)
    keep = jnp.broadcast_to(keep, (requests * spec, STAT_LANES))
    near_parts = attend(spread, [mine, *near_queries], keys, spec, heads, latent)
    near_parts, far_queries = lax.optimization_barrier((near_parts, far_queries))
    far_parts = attend(spread, [far, *far_queries], keys, spec, heads, latent)
    near_parts, far_parts = lax.optimization_barrier((near_parts, far_parts))
    far_part = combine(
        [far_parts[0]] + [swap(part, bits) for part, bits in zip(far_parts[1:], near)], latent
    )
    parts = [swap(far_part, far_bit), near_parts[0]]
    parts += [swap(part, bits) for part, bits in zip(near_parts[1:], near)]
    own, give = merge(parts, latent)
    outs = project(own, swap(give, 1), value_up, output_weight, spec, n)
    received = lax.all_to_all(outs, "ctx", 0, 0, tiled=True)
    return finish(received, keep, requests)


def solution(mesh):
    return jax.shard_map(
        functools.partial(on_device, mesh.shape["ctx"]),
        mesh=mesh,
        in_specs=(
            P("grp", None, "ctx", None),
            P("grp", "ctx", None),
            P("grp"),
            P("grp", None),
            P("ctx", None, None),
            P("ctx", None),
        ),
        out_specs=P("grp", None, "ctx"),
        check_vma=False,
    )
```

```python
import functools
import math

import jax
import jax.numpy as jnp
from jax import lax
from jax.experimental import pallas as pl
from jax.experimental.pallas import tpu as pltpu
from jax.sharding import PartitionSpec as P

SOFTMAX_SCALE = 192.0 ** (-0.5)
LOG2_SCALE = SOFTMAX_SCALE * math.log2(math.e)
SCORE_FLOOR = -1e30
STAT_LANES = 128
MIB = 1024 * 1024
HINT = 20 * MIB


def split_low(x):
    high = x.astype(jnp.bfloat16).astype(jnp.float32)
    return high, (x - high).astype(jnp.bfloat16).astype(jnp.float32)


def select_kernel(own_ref, got_ref, out_ref):
    core = lax.rem(lax.axis_index("ctx"), 2)
    rows = out_ref.shape[0] // 2
    out_ref[:rows] = own_ref[core].reshape(rows, -1)
    out_ref[rows:] = got_ref[core].reshape(rows, -1)


def select(own, got):
    requests, spec, heads, feature = own.shape
    return pl.pallas_call(
        select_kernel,
        out_shape=jax.ShapeDtypeStruct((2 * spec * heads, feature), own.dtype),
        compiler_params=pltpu.CompilerParams(vmem_limit_bytes=8 * MIB),
        cost_estimate=pl.CostEstimate(flops=0, bytes_accessed=HINT, transcendentals=0),
        name="select",
    )(own, got)


def attend_kernel(chunks, spec, heads, latent, lengths_ref, *refs):
    q_refs, key_refs, out_refs = refs[:chunks], refs[chunks : chunks + 2], refs[chunks + 2 :]
    block = key_refs[1].shape[1]
    width = min(block, 512)
    per_block = block // width
    steps = 2 * per_block
    me = lax.axis_index("ctx")
    bases = (me * block, (me + 1 - 2 * lax.rem(me, 2)) * block)
    queries = jnp.concatenate([ref[...] for ref in q_refs], axis=0)
    rows = queries.shape[0]
    row = lax.broadcasted_iota(jnp.int32, (rows, 1), 0)
    draft = lax.rem(lax.div(row, heads), spec)
    horizon = lengths_ref[pl.ds(lax.rem(me, 2), 1), :1] - spec + 1 + draft

    def keys(step, features):
        start = (step % per_block) * width
        if step < per_block:
            return key_refs[0][lax.rem(me, 2), :features, start : start + width]
        return key_refs[1][:features, start : start + width]

    def score(step):
        tile = jnp.dot(queries, keys(step, None), preferred_element_type=jnp.float32)
        start = bases[step // per_block] + (step % per_block) * width
        position = start + lax.broadcasted_iota(jnp.int32, (1, width), 1)
        return jnp.where(position < horizon, tile * LOG2_SCALE, SCORE_FLOOR)

    peak = jnp.full((rows, 1), 0.1 * SCORE_FLOOR, jnp.float32)
    denominator = jnp.zeros((rows, 1), jnp.float32)
    numerator = jnp.zeros((rows, latent), jnp.float32)
    tile = score(0)
    for step in range(steps):
        following = score(step + 1) if step + 1 < steps else None
        higher = jnp.maximum(peak, jnp.max(tile, axis=1, keepdims=True))
        if step == steps - 1:
            higher = sum(split_low(higher))
        weights = jnp.exp2(tile - higher)
        ratio = jnp.exp2(peak - higher)
        denominator = denominator * ratio + jnp.sum(weights, axis=1, keepdims=True)
        numerator = numerator * ratio + lax.dot_general(
            weights.astype(jnp.bfloat16),
            keys(step, latent),
            (((1,), (1,)), ((), ())),
            preferred_element_type=jnp.float32,
        )
        peak, tile = higher, following
    chunk = rows // chunks
    for i, out_ref in enumerate(out_refs):
        part = slice(i * chunk, (i + 1) * chunk)
        store_part(out_ref, latent, peak[part], denominator[part], numerator[part])


def attend(lengths, query_chunks, keys, spec, heads, latent):
    chunks = len(query_chunks)
    chunk, feature = query_chunks[0].shape
    rows, positions = chunks * chunk, 2 * keys[1].shape[1]
    return pl.pallas_call(
        functools.partial(attend_kernel, chunks, spec, heads, latent),
        out_shape=[jax.ShapeDtypeStruct((chunk, latent + STAT_LANES), jnp.bfloat16)] * chunks,
        compiler_params=pltpu.CompilerParams(vmem_limit_bytes=12 * MIB),
        cost_estimate=pl.CostEstimate(
            flops=2 * rows * positions * (feature + latent),
            bytes_accessed=2 * positions * feature,
            transcendentals=rows * positions,
        ),
        name="attend",
    )(lengths, *query_chunks, *keys)


def merged(in_refs, latent):
    peaks, denominators = [], []
    for ref in in_refs:
        stats = ref[:, latent:].astype(jnp.float32)
        peaks.append(stats[:, 0:1] + stats[:, 1:2])
        denominators.append(stats[:, 2:3] + stats[:, 3:4])
    largest = functools.reduce(jnp.maximum, peaks)
    upper, lower = 0.0, 0.0
    for ref, peak, denominator in zip(in_refs, peaks, denominators):
        factor = jnp.exp2(peak - largest)
        upper += factor * ref[:, :latent].astype(jnp.float32)
        lower += factor * denominator
    return largest, lower, upper


def store_part(ref, latent, peak, denominator, numerator):
    peak_high, peak_low = split_low(peak)
    denom_high, denom_low = split_low(denominator)
    lane = lax.broadcasted_iota(jnp.int32, (ref.shape[0], STAT_LANES), 1)
    stats = jnp.where(lane == 0, peak_high, jnp.where(lane == 1, peak_low, 0.0))
    stats = jnp.where(lane == 2, denom_high, jnp.where(lane == 3, denom_low, stats))
    ref[:, :latent] = numerator.astype(jnp.bfloat16)
    ref[:, latent:] = stats.astype(jnp.bfloat16)


def combine_kernel(parts, latent, *refs):
    store_part(refs[parts], latent, *merged(refs[:parts], latent))


def combine(parts, latent):
    return pl.pallas_call(
        functools.partial(combine_kernel, len(parts), latent),
        out_shape=jax.ShapeDtypeStruct(parts[0].shape, jnp.bfloat16),
        compiler_params=pltpu.CompilerParams(vmem_limit_bytes=8 * MIB),
        name="combine",
    )(*parts)


def merge_kernel(parts, latent, *refs):
    _, lower, upper = merged(refs[:parts], latent)
    own_ref, give_ref = refs[parts:]
    attended = (upper / lower).astype(jnp.bfloat16)
    half = attended.shape[0] // 2
    own_ref[...] = attended[:half]
    give_ref[...] = attended[half:]


def merge(parts, latent):
    rows = parts[0].shape[0]
    return pl.pallas_call(
        functools.partial(merge_kernel, len(parts), latent),
        out_shape=[jax.ShapeDtypeStruct((rows // 2, latent), jnp.bfloat16)] * 2,
        compiler_params=pltpu.CompilerParams(vmem_limit_bytes=8 * MIB),
        name="merge",
    )(*parts)


def project_kernel(heads, group, own_ref, got_ref, up_ref, weight_ref, out_ref):
    core = lax.rem(lax.axis_index("ctx"), 2)
    own, got = own_ref[...], got_ref[...]
    first = jnp.where(core == 0, own, got)
    second = jnp.where(core == 0, got, own)
    attended = jnp.concatenate([first, second], axis=0)
    rows = attended.shape[0]
    head = lax.rem(lax.broadcasted_iota(jnp.int32, (rows, 1), 0), heads)
    values = []
    for h in range(heads):
        tile = jnp.dot(attended, up_ref[h], preferred_element_type=jnp.float32)
        tile = jnp.where(head == h, tile, 0.0)
        tile = jnp.sum(tile.reshape(rows // heads, heads, tile.shape[1]), axis=1)
        values.append(tile.astype(jnp.bfloat16))
    values = jnp.concatenate(values, axis=1)
    owners, _, columns = out_ref.shape
    for i in range(0, owners, group):
        part = weight_ref[:, i * columns : (i + group) * columns]
        tile = jnp.dot(values, part, preferred_element_type=jnp.float32)
        for j in range(group):
            piece = tile[:, j * columns : (j + 1) * columns]
            out_ref[i + j] = piece.astype(out_ref.dtype)


def project(own, got, value_up, weight, spec, owners):
    heads = own.shape[0] // spec
    columns = weight.shape[1] // owners
    group = next(g for g in (2, 1, 4, 8, 16, owners) if (g * columns) % 128 == 0)
    return pl.pallas_call(
        functools.partial(project_kernel, heads, group),
        out_shape=jax.ShapeDtypeStruct((owners, 2 * spec, columns), jnp.bfloat16),
        in_specs=[pl.BlockSpec(memory_space=pltpu.VMEM)] * 4,
        out_specs=pl.BlockSpec(memory_space=pltpu.VMEM),
        compiler_params=pltpu.CompilerParams(vmem_limit_bytes=12 * MIB),
        name="project",
    )(own, got, value_up, weight)


def finish_kernel(in_ref, keep_ref, out_ref):
    total = jnp.sum(in_ref[...].astype(jnp.float32), axis=0) * keep_ref[:, :1]
    spec = out_ref.shape[1]
    for r in range(out_ref.shape[0]):
        out_ref[r] = total[r * spec : (r + 1) * spec].astype(out_ref.dtype)


def finish(parts, keep, requests):
    _, rows, columns = parts.shape
    return pl.pallas_call(
        finish_kernel,
        out_shape=jax.ShapeDtypeStruct((requests, rows // requests, columns), jnp.bfloat16),
        compiler_params=pltpu.CompilerParams(vmem_limit_bytes=8 * MIB),
        name="finish",
    )(parts, keep)


def on_device(n, queries, latent_cache, lengths, draft_mask, value_up, output_weight):
    requests, spec, heads, feature = queries.shape
    latent = value_up.shape[1]
    core = lax.rem(lax.axis_index("ctx"), 2)

    def swap(x, bits):
        return lax.ppermute(x, "ctx", [(i, i ^ bits) for i in range(n)])

    chunk = requests * spec * heads
    got = swap(queries, 1)
    mine = select(queries, got)
    own_keys = jnp.swapaxes(latent_cache, 1, 2)
    got_keys = swap(lax.optimization_barrier((own_keys, got))[0], 1)

    far_bit = n // 2
    near = [2 * k for k in range(1, n // 4)][::-1]
    far = swap(mine, far_bit)
    near_queries = [swap(mine, bits) for bits in near]

    draft_mask = lax.optimization_barrier((draft_mask, mine))[0]
    keys = [own_keys, lax.dynamic_index_in_dim(got_keys, core, 0, keepdims=False)]
    far, near_queries[2] = lax.optimization_barrier((far, near_queries[2]))
    far_queries = [swap(far, bits) for bits in near]
    spread = jnp.broadcast_to(lengths[:, None], (requests, STAT_LANES))
    keep = draft_mask.astype(jnp.float32).reshape(requests * spec, 1)
    keep = jnp.broadcast_to(keep, (requests * spec, STAT_LANES))
    near_parts = attend(spread, [mine, *near_queries], keys, spec, heads, latent)
    near_parts, far_queries = lax.optimization_barrier((near_parts, far_queries))
    far_parts = attend(spread, [far, *far_queries], keys, spec, heads, latent)
    near_parts, far_parts = lax.optimization_barrier((near_parts, far_parts))
    far_part = combine(
        [far_parts[0]] + [swap(part, bits) for part, bits in zip(far_parts[1:], near)], latent
    )
    parts = [swap(far_part, far_bit), near_parts[0]]
    parts += [swap(part, bits) for part, bits in zip(near_parts[1:], near)]
    own, give = merge(parts, latent)
    outs = project(own, swap(give, 1), value_up, output_weight, spec, n)
    received = lax.all_to_all(outs, "ctx", 0, 0, tiled=True)
    return finish(received, keep, requests)


def solution(mesh):
    return jax.shard_map(
        functools.partial(on_device, mesh.shape["ctx"]),
        mesh=mesh,
        in_specs=(
            P("grp", None, "ctx", None),
            P("grp", "ctx", None),
            P("grp"),
            P("grp", None),
            P("ctx", None, None),
            P("ctx", None),
        ),
        out_specs=P("grp", None, "ctx"),
        check_vma=False,
    )
```

```python
import functools
import math

import jax
import jax.numpy as jnp
from jax import lax
from jax.experimental import pallas as pl
from jax.experimental.pallas import tpu as pltpu
from jax.sharding import PartitionSpec as P

SOFTMAX_SCALE = 192.0 ** (-0.5)
LOG2_SCALE = SOFTMAX_SCALE * math.log2(math.e)
SCORE_FLOOR = -1e30
STAT_LANES = 128
MIB = 1024 * 1024
HINT = 20 * MIB


def split_low(x):
    high = x.astype(jnp.bfloat16).astype(jnp.float32)
    return high, (x - high).astype(jnp.bfloat16).astype(jnp.float32)


def select_kernel(own_ref, got_ref, out_ref):
    core = lax.rem(lax.axis_index("ctx"), 2)
    rows = out_ref.shape[0] // 2
    out_ref[:rows] = own_ref[...].reshape(rows, -1)
    out_ref[rows:] = got_ref[core].reshape(rows, -1)


def select(own, got):
    spec, heads, feature = own.shape
    return pl.pallas_call(
        select_kernel,
        out_shape=jax.ShapeDtypeStruct((2 * spec * heads, feature), own.dtype),
        compiler_params=pltpu.CompilerParams(vmem_limit_bytes=8 * MIB),
        cost_estimate=pl.CostEstimate(flops=0, bytes_accessed=HINT, transcendentals=0),
        name="select",
    )(own, got)


def attend_kernel(chunks, spec, heads, latent, lengths_ref, *refs):
    q_refs, key_refs, out_refs = refs[:chunks], refs[chunks : chunks + 2], refs[chunks + 2 :]
    block = key_refs[1].shape[1]
    width = min(block, 512)
    per_block = block // width
    steps = 2 * per_block
    me = lax.axis_index("ctx")
    bases = (me * block, (me + 1 - 2 * lax.rem(me, 2)) * block)
    queries = jnp.concatenate([ref[...] for ref in q_refs], axis=0)
    rows = queries.shape[0]
    row = lax.broadcasted_iota(jnp.int32, (rows, 1), 0)
    draft = lax.rem(lax.div(row, heads), spec)
    horizon = lengths_ref[pl.ds(lax.rem(me, 2), 1), :1] - spec + 1 + draft

    def keys(step, features):
        start = (step % per_block) * width
        if step < per_block:
            return key_refs[0][lax.rem(me, 2), :features, start : start + width]
        return key_refs[1][:features, start : start + width]

    def score(step):
        tile = jnp.dot(queries, keys(step, None), preferred_element_type=jnp.float32)
        start = bases[step // per_block] + (step % per_block) * width
        position = start + lax.broadcasted_iota(jnp.int32, (1, width), 1)
        return jnp.where(position < horizon, tile * LOG2_SCALE, SCORE_FLOOR)

    peak = jnp.full((rows, 1), 0.1 * SCORE_FLOOR, jnp.float32)
    denominator = jnp.zeros((rows, 1), jnp.float32)
    numerator = jnp.zeros((rows, latent), jnp.float32)
    tile = score(0)
    for step in range(steps):
        following = score(step + 1) if step + 1 < steps else None
        higher = jnp.maximum(peak, jnp.max(tile, axis=1, keepdims=True))
        if step == steps - 1:
            higher = sum(split_low(higher))
        weights = jnp.exp2(tile - higher)
        ratio = jnp.exp2(peak - higher)
        denominator = denominator * ratio + jnp.sum(weights, axis=1, keepdims=True)
        numerator = numerator * ratio + lax.dot_general(
            weights.astype(jnp.bfloat16),
            keys(step, latent),
            (((1,), (1,)), ((), ())),
            preferred_element_type=jnp.float32,
        )
        peak, tile = higher, following
    chunk = rows // chunks
    for i, out_ref in enumerate(out_refs):
        part = slice(i * chunk, (i + 1) * chunk)
        store_part(out_ref, latent, peak[part], denominator[part], numerator[part])


def attend(lengths, query_chunks, keys, spec, heads, latent):
    chunks = len(query_chunks)
    chunk, feature = query_chunks[0].shape
    rows, positions = chunks * chunk, 2 * keys[1].shape[1]
    return pl.pallas_call(
        functools.partial(attend_kernel, chunks, spec, heads, latent),
        out_shape=[jax.ShapeDtypeStruct((chunk, latent + STAT_LANES), jnp.bfloat16)] * chunks,
        compiler_params=pltpu.CompilerParams(vmem_limit_bytes=12 * MIB),
        cost_estimate=pl.CostEstimate(
            flops=2 * rows * positions * (feature + latent),
            bytes_accessed=2 * positions * feature,
            transcendentals=rows * positions,
        ),
        name="attend",
    )(lengths, *query_chunks, *keys)


def merged(in_refs, latent):
    peaks, denominators = [], []
    for ref in in_refs:
        stats = ref[:, latent:].astype(jnp.float32)
        peaks.append(stats[:, 0:1] + stats[:, 1:2])
        denominators.append(stats[:, 2:3] + stats[:, 3:4])
    largest = functools.reduce(jnp.maximum, peaks)
    upper, lower = 0.0, 0.0
    for ref, peak, denominator in zip(in_refs, peaks, denominators):
        factor = jnp.exp2(peak - largest)
        upper += factor * ref[:, :latent].astype(jnp.float32)
        lower += factor * denominator
    return largest, lower, upper


def store_part(ref, latent, peak, denominator, numerator):
    peak_high, peak_low = split_low(peak)
    denom_high, denom_low = split_low(denominator)
    lane = lax.broadcasted_iota(jnp.int32, (ref.shape[0], STAT_LANES), 1)
    stats = jnp.where(lane == 0, peak_high, jnp.where(lane == 1, peak_low, 0.0))
    stats = jnp.where(lane == 2, denom_high, jnp.where(lane == 3, denom_low, stats))
    ref[:, :latent] = numerator.astype(jnp.bfloat16)
    ref[:, latent:] = stats.astype(jnp.bfloat16)


def combine_kernel(parts, latent, *refs):
    store_part(refs[parts], latent, *merged(refs[:parts], latent))


def combine(parts, latent):
    return pl.pallas_call(
        functools.partial(combine_kernel, len(parts), latent),
        out_shape=jax.ShapeDtypeStruct(parts[0].shape, jnp.bfloat16),
        compiler_params=pltpu.CompilerParams(vmem_limit_bytes=8 * MIB),
        name="combine",
    )(*parts)


def merge_kernel(parts, latent, *refs):
    _, lower, upper = merged(refs[:parts], latent)
    own_ref, give_ref = refs[parts:]
    attended = (upper / lower).astype(jnp.bfloat16)
    half = attended.shape[0] // 2
    own_ref[...] = attended[:half]
    give_ref[...] = attended[half:]


def merge(parts, latent):
    rows = parts[0].shape[0]
    return pl.pallas_call(
        functools.partial(merge_kernel, len(parts), latent),
        out_shape=[jax.ShapeDtypeStruct((rows // 2, latent), jnp.bfloat16)] * 2,
        compiler_params=pltpu.CompilerParams(vmem_limit_bytes=8 * MIB),
        name="merge",
    )(*parts)


def project_kernel(heads, group, own_ref, got_ref, up_ref, weight_ref, out_ref, sums_ref):
    core = lax.rem(lax.axis_index("ctx"), 2)
    own, got = own_ref[...], got_ref[...]
    first = jnp.where(core == 0, own, got)
    second = jnp.where(core == 0, got, own)
    attended = jnp.concatenate([first, second], axis=0)
    rows = attended.shape[0]
    head = lax.rem(lax.broadcasted_iota(jnp.int32, (rows, 1), 0), heads)
    values = []
    for h in range(heads):
        tile = jnp.dot(attended, up_ref[h], preferred_element_type=jnp.float32)
        tile = jnp.where(head == h, tile, 0.0)
        tile = jnp.sum(tile.reshape(rows // heads, heads, tile.shape[1]), axis=1)
        values.append(tile.astype(jnp.bfloat16))
    values = jnp.concatenate(values, axis=1)
    owners, _, columns = out_ref.shape
    for i in range(0, owners, group):
        part = weight_ref[:, i * columns : (i + group) * columns]
        tile = jnp.dot(values, part, preferred_element_type=jnp.float32)
        for j in range(group):
            sums_ref[i + j] = tile[:, j * columns : (j + 1) * columns]
    out_ref[...] = sums_ref[...].astype(out_ref.dtype)


def project(own, got, value_up, weight, spec, owners):
    heads = own.shape[0] // spec
    columns = weight.shape[1] // owners
    group = next(g for g in (2, 1, 4, 8, 16, owners) if (g * columns) % 128 == 0)
    return pl.pallas_call(
        functools.partial(project_kernel, heads, group),
        out_shape=jax.ShapeDtypeStruct((owners, 2 * spec, columns), jnp.bfloat16),
        in_specs=[pl.BlockSpec(memory_space=pltpu.VMEM)] * 4,
        out_specs=pl.BlockSpec(memory_space=pltpu.VMEM),
        scratch_shapes=[pltpu.VMEM((owners, 2 * spec, columns), jnp.float32)],
        compiler_params=pltpu.CompilerParams(vmem_limit_bytes=12 * MIB),
        name="project",
    )(own, got, value_up, weight)


def finish_kernel(in_ref, keep_ref, out_ref):
    total = jnp.sum(in_ref[...].astype(jnp.float32), axis=0) * keep_ref[:, :1]
    spec = out_ref.shape[1]
    for r in range(out_ref.shape[0]):
        out_ref[r] = total[r * spec : (r + 1) * spec].astype(out_ref.dtype)


def finish(parts, keep, requests):
    _, rows, columns = parts.shape
    return pl.pallas_call(
        finish_kernel,
        out_shape=jax.ShapeDtypeStruct((requests, rows // requests, columns), jnp.bfloat16),
        compiler_params=pltpu.CompilerParams(vmem_limit_bytes=8 * MIB),
        name="finish",
    )(parts, keep)


def on_device(n, queries, latent_cache, lengths, draft_mask, value_up, output_weight):
    requests, spec, heads, feature = queries.shape
    latent = value_up.shape[1]
    core = lax.rem(lax.axis_index("ctx"), 2)

    def swap(x, bits):
        return lax.ppermute(x, "ctx", [(i, i ^ bits) for i in range(n)])

    chunk = requests * spec * heads
    got = swap(queries, 1)
    own_queries = lax.dynamic_index_in_dim(queries, core, 0, keepdims=False)
    own_queries, got = lax.optimization_barrier((own_queries, got))
    mine = select(own_queries, got)
    own_keys = jnp.swapaxes(latent_cache, 1, 2)
    got_keys = swap(lax.optimization_barrier((own_keys, got))[0], 1)

    far_bit = n // 2
    near = [2 * k for k in range(1, n // 4)][::-1]
    far = swap(mine, far_bit)
    near_queries = [swap(mine, bits) for bits in near]

    draft_mask = lax.optimization_barrier((draft_mask, mine))[0]
    keys = [own_keys, lax.dynamic_index_in_dim(got_keys, core, 0, keepdims=False)]
    far, near_queries[2] = lax.optimization_barrier((far, near_queries[2]))
    far_queries = [swap(far, bits) for bits in near]
    spread = jnp.broadcast_to(lengths[:, None], (requests, STAT_LANES))
    keep = draft_mask.astype(jnp.float32).reshape(requests * spec, 1)
    keep = jnp.broadcast_to(keep, (requests * spec, STAT_LANES))
    near_parts = attend(spread, [mine, *near_queries], keys, spec, heads, latent)
    near_parts, far_queries = lax.optimization_barrier((near_parts, far_queries))
    far_parts = attend(spread, [far, *far_queries], keys, spec, heads, latent)
    near_parts, far_parts = lax.optimization_barrier((near_parts, far_parts))
    far_part = combine(
        [far_parts[0]] + [swap(part, bits) for part, bits in zip(far_parts[1:], near)], latent
    )
    parts = [swap(far_part, far_bit), near_parts[0]]
    parts += [swap(part, bits) for part, bits in zip(near_parts[1:], near)]
    own, give = merge(parts, latent)
    outs = project(own, swap(give, 1), value_up, output_weight, spec, n)
    received = lax.all_to_all(outs, "ctx", 0, 0, tiled=True)
    return finish(received, keep, requests)


def solution(mesh):
    return jax.shard_map(
        functools.partial(on_device, mesh.shape["ctx"]),
        mesh=mesh,
        in_specs=(
            P("grp", None, "ctx", None),
            P("grp", "ctx", None),
            P("grp"),
            P("grp", None),
            P("ctx", None, None),
            P("ctx", None),
        ),
        out_specs=P("grp", None, "ctx"),
        check_vma=False,
    )
```

```python
import functools
import math

import jax
import jax.numpy as jnp
from jax import lax
from jax.experimental import pallas as pl
from jax.experimental.pallas import tpu as pltpu
from jax.sharding import PartitionSpec as P

SOFTMAX_SCALE = 192.0 ** (-0.5)
LOG2_SCALE = SOFTMAX_SCALE * math.log2(math.e)
SCORE_FLOOR = -1e30
STAT_LANES = 128
MIB = 1024 * 1024
HINT = 20 * MIB


def split_low(x):
    high = x.astype(jnp.bfloat16).astype(jnp.float32)
    return high, (x - high).astype(jnp.bfloat16).astype(jnp.float32)


def select_kernel(own_ref, got_ref, out_ref):
    core = lax.rem(lax.axis_index("ctx"), 2)
    rows = out_ref.shape[0] // 2
    out_ref[:rows] = own_ref[...].reshape(rows, -1)
    out_ref[rows:] = got_ref[core].reshape(rows, -1)


def select(own, got):
    spec, heads, feature = own.shape
    return pl.pallas_call(
        select_kernel,
        out_shape=jax.ShapeDtypeStruct((2 * spec * heads, feature), own.dtype),
        compiler_params=pltpu.CompilerParams(vmem_limit_bytes=8 * MIB),
        cost_estimate=pl.CostEstimate(flops=0, bytes_accessed=HINT, transcendentals=0),
        name="select",
    )(own, got)


def attend_kernel(chunks, spec, heads, latent, lengths_ref, mask_ref, *refs):
    q_refs, key_refs, out_refs = refs[:chunks], refs[chunks : chunks + 2], refs[chunks + 2 :]
    block = key_refs[1].shape[1]
    width = min(block, 512)
    per_block = block // width
    steps = 2 * per_block
    me = lax.axis_index("ctx")
    bases = (me * block, (me + 1 - 2 * lax.rem(me, 2)) * block)
    queries = jnp.concatenate([ref[...] for ref in q_refs], axis=0)
    rows = queries.shape[0]
    row = lax.broadcasted_iota(jnp.int32, (rows, 1), 0)
    draft = lax.rem(lax.div(row, heads), spec)
    horizon = lengths_ref[pl.ds(lax.rem(me, 2), 1), :1] - spec + 1 + draft

    def keys(step, features):
        start = (step % per_block) * width
        if step < per_block:
            return key_refs[0][lax.rem(me, 2), :features, start : start + width]
        return key_refs[1][:features, start : start + width]

    def score(step):
        tile = jnp.dot(queries, keys(step, None), preferred_element_type=jnp.float32)
        start = bases[step // per_block] + (step % per_block) * width
        position = start + lax.broadcasted_iota(jnp.int32, (1, width), 1)
        return jnp.where(position < horizon, tile * LOG2_SCALE, SCORE_FLOOR)

    peak = jnp.full((rows, 1), 0.1 * SCORE_FLOOR, jnp.float32)
    denominator = jnp.zeros((rows, 1), jnp.float32)
    numerator = jnp.zeros((rows, latent), jnp.float32)
    tile = score(0)
    for step in range(steps):
        following = score(step + 1) if step + 1 < steps else None
        higher = jnp.maximum(peak, jnp.max(tile, axis=1, keepdims=True))
        if step == steps - 1:
            higher = sum(split_low(higher))
        weights = jnp.exp2(tile - higher)
        ratio = jnp.exp2(peak - higher)
        denominator = denominator * ratio + jnp.sum(weights, axis=1, keepdims=True)
        numerator = numerator * ratio + lax.dot_general(
            weights.astype(jnp.bfloat16),
            keys(step, latent),
            (((1,), (1,)), ((), ())),
            preferred_element_type=jnp.float32,
        )
        peak, tile = higher, following
    mask = mask_ref[pl.ds(lax.rem(me, 2), 1), :].astype(jnp.float32)
    numerator *= sum(jnp.where(draft == j, mask[:, j : j + 1], 0.0) for j in range(spec))
    chunk = rows // chunks
    for i, out_ref in enumerate(out_refs):
        part = slice(i * chunk, (i + 1) * chunk)
        store_part(out_ref, latent, peak[part], denominator[part], numerator[part])


def attend(lengths, mask, query_chunks, keys, spec, heads, latent):
    chunks = len(query_chunks)
    chunk, feature = query_chunks[0].shape
    rows, positions = chunks * chunk, 2 * keys[1].shape[1]
    return pl.pallas_call(
        functools.partial(attend_kernel, chunks, spec, heads, latent),
        out_shape=[jax.ShapeDtypeStruct((chunk, latent + STAT_LANES), jnp.bfloat16)] * chunks,
        compiler_params=pltpu.CompilerParams(vmem_limit_bytes=12 * MIB),
        cost_estimate=pl.CostEstimate(
            flops=2 * rows * positions * (feature + latent),
            bytes_accessed=2 * positions * feature,
            transcendentals=rows * positions,
        ),
        name="attend",
    )(lengths, mask, *query_chunks, *keys)


def merged(in_refs, latent):
    peaks, denominators = [], []
    for ref in in_refs:
        stats = ref[:, latent:].astype(jnp.float32)
        peaks.append(stats[:, 0:1] + stats[:, 1:2])
        denominators.append(stats[:, 2:3] + stats[:, 3:4])
    largest = functools.reduce(jnp.maximum, peaks)
    upper, lower = 0.0, 0.0
    for ref, peak, denominator in zip(in_refs, peaks, denominators):
        factor = jnp.exp2(peak - largest)
        upper += factor * ref[:, :latent].astype(jnp.float32)
        lower += factor * denominator
    return largest, lower, upper


def store_part(ref, latent, peak, denominator, numerator):
    peak_high, peak_low = split_low(peak)
    denom_high, denom_low = split_low(denominator)
    lane = lax.broadcasted_iota(jnp.int32, (ref.shape[0], STAT_LANES), 1)
    stats = jnp.where(lane == 0, peak_high, jnp.where(lane == 1, peak_low, 0.0))
    stats = jnp.where(lane == 2, denom_high, jnp.where(lane == 3, denom_low, stats))
    ref[:, :latent] = numerator.astype(jnp.bfloat16)
    ref[:, latent:] = stats.astype(jnp.bfloat16)


def combine_kernel(parts, latent, *refs):
    store_part(refs[parts], latent, *merged(refs[:parts], latent))


def combine(parts, latent):
    return pl.pallas_call(
        functools.partial(combine_kernel, len(parts), latent),
        out_shape=jax.ShapeDtypeStruct(parts[0].shape, jnp.bfloat16),
        compiler_params=pltpu.CompilerParams(vmem_limit_bytes=8 * MIB),
        name="combine",
    )(*parts)


def merge_kernel(parts, latent, *refs):
    _, lower, upper = merged(refs[:parts], latent)
    own_ref, give_ref = refs[parts:]
    attended = (upper / lower).astype(jnp.bfloat16)
    half = attended.shape[0] // 2
    own_ref[...] = attended[:half]
    give_ref[...] = attended[half:]


def merge(parts, latent):
    rows = parts[0].shape[0]
    return pl.pallas_call(
        functools.partial(merge_kernel, len(parts), latent),
        out_shape=[jax.ShapeDtypeStruct((rows // 2, latent), jnp.bfloat16)] * 2,
        compiler_params=pltpu.CompilerParams(vmem_limit_bytes=8 * MIB),
        name="merge",
    )(*parts)


def project_kernel(heads, group, own_ref, got_ref, up_ref, weight_ref, out_ref):
    core = lax.rem(lax.axis_index("ctx"), 2)
    own, got = own_ref[...], got_ref[...]
    first = jnp.where(core == 0, own, got)
    second = jnp.where(core == 0, got, own)
    attended = jnp.concatenate([first, second], axis=0)
    rows = attended.shape[0]
    head = lax.rem(lax.broadcasted_iota(jnp.int32, (rows, 1), 0), heads)
    values = []
    for h in range(heads):
        tile = jnp.dot(attended, up_ref[h], preferred_element_type=jnp.float32)
        tile = jnp.where(head == h, tile, 0.0)
        tile = jnp.sum(tile.reshape(rows // heads, heads, tile.shape[1]), axis=1)
        values.append(tile.astype(jnp.bfloat16))
    values = jnp.concatenate(values, axis=1)
    owners, _, columns = out_ref.shape
    for i in range(0, owners, group):
        part = weight_ref[:, i * columns : (i + group) * columns]
        tile = jnp.dot(values, part, preferred_element_type=jnp.float32)
        for j in range(group):
            piece = tile[:, j * columns : (j + 1) * columns]
            out_ref[i + j] = piece.astype(out_ref.dtype)


def project(own, got, value_up, weight, spec, owners):
    heads = own.shape[0] // spec
    columns = weight.shape[1] // owners
    group = next(g for g in (2, 1, 4, 8, 16, owners) if (g * columns) % 128 == 0)
    return pl.pallas_call(
        functools.partial(project_kernel, heads, group),
        out_shape=jax.ShapeDtypeStruct((owners, 2 * spec, columns), jnp.bfloat16),
        in_specs=[pl.BlockSpec(memory_space=pltpu.VMEM)] * 4,
        out_specs=pl.BlockSpec(memory_space=pltpu.VMEM),
        compiler_params=pltpu.CompilerParams(vmem_limit_bytes=12 * MIB),
        name="project",
    )(own, got, value_up, weight)


def finish_kernel(in_ref, out_ref):
    total = jnp.sum(in_ref[...].astype(jnp.float32), axis=0)
    spec = out_ref.shape[1]
    for r in range(out_ref.shape[0]):
        out_ref[r] = total[r * spec : (r + 1) * spec].astype(out_ref.dtype)


def finish(parts, requests):
    _, rows, columns = parts.shape
    return pl.pallas_call(
        finish_kernel,
        out_shape=jax.ShapeDtypeStruct((requests, rows // requests, columns), jnp.bfloat16),
        compiler_params=pltpu.CompilerParams(vmem_limit_bytes=8 * MIB),
        name="finish",
    )(parts)


def on_device(n, queries, latent_cache, lengths, draft_mask, value_up, output_weight):
    requests, spec, heads, feature = queries.shape
    latent = value_up.shape[1]
    core = lax.rem(lax.axis_index("ctx"), 2)

    def swap(x, bits):
        return lax.ppermute(x, "ctx", [(i, i ^ bits) for i in range(n)])

    chunk = requests * spec * heads
    got = swap(queries, 1)
    own_queries = lax.dynamic_index_in_dim(queries, core, 0, keepdims=False)
    own_queries, got = lax.optimization_barrier((own_queries, got))
    mine = select(own_queries, got)
    own_keys = jnp.swapaxes(latent_cache, 1, 2)
    got_keys = swap(lax.optimization_barrier((own_keys, got))[0], 1)

    far_bit = n // 2
    near = [2 * k for k in range(1, n // 4)][::-1]
    far = swap(mine, far_bit)
    near_queries = [swap(mine, bits) for bits in near]

    keys = [own_keys, lax.dynamic_index_in_dim(got_keys, core, 0, keepdims=False)]
    far, near_queries[2] = lax.optimization_barrier((far, near_queries[2]))
    far_queries = [swap(far, bits) for bits in near]
    spread = jnp.broadcast_to(lengths[:, None], (requests, STAT_LANES))
    near_parts = attend(spread, draft_mask, [mine, *near_queries], keys, spec, heads, latent)
    near_parts, far_queries = lax.optimization_barrier((near_parts, far_queries))
    far_parts = attend(spread, draft_mask, [far, *far_queries], keys, spec, heads, latent)
    near_parts, far_parts = lax.optimization_barrier((near_parts, far_parts))
    far_part = combine(
        [far_parts[0]] + [swap(part, bits) for part, bits in zip(far_parts[1:], near)], latent
    )
    parts = [swap(far_part, far_bit), near_parts[0]]
    parts += [swap(part, bits) for part, bits in zip(near_parts[1:], near)]
    own, give = merge(parts, latent)
    outs = project(own, swap(give, 1), value_up, output_weight, spec, n)
    received = lax.all_to_all(outs, "ctx", 0, 0, tiled=True)
    return finish(received, requests)


def solution(mesh):
    return jax.shard_map(
        functools.partial(on_device, mesh.shape["ctx"]),
        mesh=mesh,
        in_specs=(
            P("grp", None, "ctx", None),
            P("grp", "ctx", None),
            P("grp"),
            P("grp", None),
            P("ctx", None, None),
            P("ctx", None),
        ),
        out_specs=P("grp", None, "ctx"),
        check_vma=False,
    )
```

```python
import functools
import math

import jax
import jax.numpy as jnp
from jax import lax
from jax.experimental import pallas as pl
from jax.experimental.pallas import tpu as pltpu
from jax.sharding import PartitionSpec as P

SOFTMAX_SCALE = 192.0 ** (-0.5)
LOG2_SCALE = SOFTMAX_SCALE * math.log2(math.e)
SCORE_FLOOR = -1e30
STAT_LANES = 128
MIB = 1024 * 1024
HINT = 20 * MIB


def split_low(x):
    high = x.astype(jnp.bfloat16).astype(jnp.float32)
    return high, (x - high).astype(jnp.bfloat16).astype(jnp.float32)


def select_kernel(own_ref, got_ref, out_ref):
    core = lax.rem(lax.axis_index("ctx"), 2)
    rows = out_ref.shape[0] // 2
    out_ref[:rows] = own_ref[...].reshape(rows, -1)
    out_ref[rows:] = got_ref[core].reshape(rows, -1)


def select(own, got):
    spec, heads, feature = own.shape
    return pl.pallas_call(
        select_kernel,
        out_shape=jax.ShapeDtypeStruct((2 * spec * heads, feature), own.dtype),
        compiler_params=pltpu.CompilerParams(vmem_limit_bytes=8 * MIB),
        cost_estimate=pl.CostEstimate(flops=0, bytes_accessed=HINT, transcendentals=0),
        name="select",
    )(own, got)


def attend_kernel(chunks, spec, heads, latent, lengths_ref, mask_ref, *refs):
    q_refs, key_refs, out_refs = refs[:chunks], refs[chunks : chunks + 2], refs[chunks + 2 :]
    block = key_refs[1].shape[1]
    width = min(block, 512)
    per_block = block // width
    steps = 2 * per_block
    me = lax.axis_index("ctx")
    bases = (me * block, (me + 1 - 2 * lax.rem(me, 2)) * block)
    queries = jnp.concatenate([ref[...] for ref in q_refs], axis=0)
    rows = queries.shape[0]
    row = lax.broadcasted_iota(jnp.int32, (rows, 1), 0)
    draft = lax.rem(lax.div(row, heads), spec)
    horizon = lengths_ref[pl.ds(lax.rem(me, 2), 1), :1] - spec + 1 + draft

    def keys(step, features):
        start = (step % per_block) * width
        if step < per_block:
            return key_refs[0][lax.rem(me, 2), :features, start : start + width]
        return key_refs[1][:features, start : start + width]

    def score(step):
        tile = jnp.dot(queries, keys(step, None), preferred_element_type=jnp.float32)
        start = bases[step // per_block] + (step % per_block) * width
        position = start + lax.broadcasted_iota(jnp.int32, (1, width), 1)
        return jnp.where(position < horizon, tile * LOG2_SCALE, SCORE_FLOOR)

    peak = jnp.full((rows, 1), 0.1 * SCORE_FLOOR, jnp.float32)
    denominator = jnp.zeros((rows, 1), jnp.float32)
    numerator = jnp.zeros((rows, latent), jnp.float32)
    tile = score(0)
    for step in range(steps):
        following = score(step + 1) if step + 1 < steps else None
        higher = jnp.maximum(peak, jnp.max(tile, axis=1, keepdims=True))
        if step == steps - 1:
            higher = sum(split_low(higher))
        weights = jnp.exp2(tile - higher)
        ratio = jnp.exp2(peak - higher)
        denominator = denominator * ratio + jnp.sum(weights, axis=1, keepdims=True)
        numerator = numerator * ratio + lax.dot_general(
            weights.astype(jnp.bfloat16),
            keys(step, latent),
            (((1,), (1,)), ((), ())),
            preferred_element_type=jnp.float32,
        )
        peak, tile = higher, following
    mask = mask_ref[pl.ds(lax.rem(me, 2), 1), :].astype(jnp.float32)
    numerator *= sum(jnp.where(draft == j, mask[:, j : j + 1], 0.0) for j in range(spec))
    chunk = rows // chunks
    for i, out_ref in enumerate(out_refs):
        part = slice(i * chunk, (i + 1) * chunk)
        store_part(out_ref, latent, peak[part], denominator[part], numerator[part])


def attend(lengths, mask, query_chunks, keys, spec, heads, latent):
    chunks = len(query_chunks)
    chunk, feature = query_chunks[0].shape
    rows, positions = chunks * chunk, 2 * keys[1].shape[1]
    return pl.pallas_call(
        functools.partial(attend_kernel, chunks, spec, heads, latent),
        out_shape=[jax.ShapeDtypeStruct((chunk, latent + STAT_LANES), jnp.bfloat16)] * chunks,
        compiler_params=pltpu.CompilerParams(vmem_limit_bytes=12 * MIB),
        cost_estimate=pl.CostEstimate(
            flops=2 * rows * positions * (feature + latent),
            bytes_accessed=2 * positions * feature,
            transcendentals=rows * positions,
        ),
        name="attend",
    )(lengths, mask, *query_chunks, *keys)


def merged(in_refs, latent):
    peaks, denominators = [], []
    for ref in in_refs:
        stats = ref[:, latent:].astype(jnp.float32)
        peaks.append(stats[:, 0:1] + stats[:, 1:2])
        denominators.append(stats[:, 2:3] + stats[:, 3:4])
    largest = functools.reduce(jnp.maximum, peaks)
    upper, lower = 0.0, 0.0
    for ref, peak, denominator in zip(in_refs, peaks, denominators):
        factor = jnp.exp2(peak - largest)
        upper += factor * ref[:, :latent].astype(jnp.float32)
        lower += factor * denominator
    return largest, lower, upper


def store_part(ref, latent, peak, denominator, numerator):
    peak_high, peak_low = split_low(peak)
    denom_high, denom_low = split_low(denominator)
    lane = lax.broadcasted_iota(jnp.int32, (ref.shape[0], STAT_LANES), 1)
    stats = jnp.where(lane == 0, peak_high, jnp.where(lane == 1, peak_low, 0.0))
    stats = jnp.where(lane == 2, denom_high, jnp.where(lane == 3, denom_low, stats))
    ref[:, :latent] = numerator.astype(jnp.bfloat16)
    ref[:, latent:] = stats.astype(jnp.bfloat16)


def combine_kernel(parts, latent, *refs):
    store_part(refs[parts], latent, *merged(refs[:parts], latent))


def combine(parts, latent):
    return pl.pallas_call(
        functools.partial(combine_kernel, len(parts), latent),
        out_shape=jax.ShapeDtypeStruct(parts[0].shape, jnp.bfloat16),
        compiler_params=pltpu.CompilerParams(vmem_limit_bytes=8 * MIB),
        name="combine",
    )(*parts)


def merge_kernel(parts, latent, *refs):
    _, lower, upper = merged(refs[:parts], latent)
    own_ref, give_ref = refs[parts:]
    attended = (upper / lower).astype(jnp.bfloat16)
    half = attended.shape[0] // 2
    own_ref[...] = attended[:half]
    give_ref[...] = attended[half:]


def merge(parts, latent):
    rows = parts[0].shape[0]
    return pl.pallas_call(
        functools.partial(merge_kernel, len(parts), latent),
        out_shape=[jax.ShapeDtypeStruct((rows // 2, latent), jnp.bfloat16)] * 2,
        compiler_params=pltpu.CompilerParams(vmem_limit_bytes=8 * MIB),
        name="merge",
    )(*parts)


def project_kernel(heads, group, own_ref, got_ref, up_ref, weight_ref, out_ref):
    core = lax.rem(lax.axis_index("ctx"), 2)
    own, got = own_ref[...], got_ref[...]
    first = jnp.where(core == 0, own, got)
    second = jnp.where(core == 0, got, own)
    attended = jnp.concatenate([first, second], axis=0)
    rows = attended.shape[0]
    head = lax.rem(lax.broadcasted_iota(jnp.int32, (rows, 1), 0), heads)
    values = []
    for h in range(heads):
        tile = jnp.dot(attended, up_ref[h], preferred_element_type=jnp.float32)
        tile = jnp.where(head == h, tile, 0.0)
        tile = jnp.sum(tile.reshape(rows // heads, heads, tile.shape[1]), axis=1)
        values.append(tile.astype(jnp.bfloat16))
    values = jnp.concatenate(values, axis=1)
    owners, _, columns = out_ref.shape
    for i in range(0, owners, group):
        part = weight_ref[:, i * columns : (i + group) * columns]
        tile = jnp.dot(values, part, preferred_element_type=jnp.float32)
        for j in range(group):
            piece = tile[:, j * columns : (j + 1) * columns]
            out_ref[i + j] = piece.astype(out_ref.dtype)


def project(own, got, value_up, weight, spec, owners):
    heads = own.shape[0] // spec
    columns = weight.shape[1] // owners
    group = next(g for g in (2, 1, 4, 8, 16, owners) if (g * columns) % 128 == 0)
    return pl.pallas_call(
        functools.partial(project_kernel, heads, group),
        out_shape=jax.ShapeDtypeStruct((owners, 2 * spec, columns), jnp.bfloat16),
        in_specs=[pl.BlockSpec(memory_space=pltpu.VMEM)] * 4,
        out_specs=pl.BlockSpec(memory_space=pltpu.VMEM),
        compiler_params=pltpu.CompilerParams(vmem_limit_bytes=12 * MIB),
        name="project",
    )(own, got, value_up, weight)


def finish_kernel(in_ref, out_ref):
    total = jnp.sum(in_ref[...].astype(jnp.float32), axis=0)
    spec = out_ref.shape[1]
    for r in range(out_ref.shape[0]):
        out_ref[r] = total[r * spec : (r + 1) * spec].astype(out_ref.dtype)


def finish(parts, requests):
    _, rows, columns = parts.shape
    return pl.pallas_call(
        finish_kernel,
        out_shape=jax.ShapeDtypeStruct((requests, rows // requests, columns), jnp.bfloat16),
        compiler_params=pltpu.CompilerParams(vmem_limit_bytes=8 * MIB),
        name="finish",
    )(parts)


def on_device(n, queries, latent_cache, lengths, draft_mask, value_up, output_weight):
    requests, spec, heads, feature = queries.shape
    latent = value_up.shape[1]
    core = lax.rem(lax.axis_index("ctx"), 2)

    def swap(x, bits):
        return lax.ppermute(x, "ctx", [(i, i ^ bits) for i in range(n)])

    chunk = requests * spec * heads
    got = swap(queries, 1)
    own_queries = lax.dynamic_index_in_dim(queries, core, 0, keepdims=False)
    own_queries, got = lax.optimization_barrier((own_queries, got))
    mine = select(own_queries, got)
    own_keys = jnp.swapaxes(latent_cache, 1, 2)
    got_keys = swap(lax.optimization_barrier((own_keys, got))[0], 1)

    far_bit = n // 2
    near = [2 * k for k in range(1, n // 4)][::-1]
    far = swap(mine, far_bit)
    near_queries = [swap(mine, bits) for bits in near]

    keys = [own_keys, lax.dynamic_index_in_dim(got_keys, core, 0, keepdims=False)]
    far, near_queries[2] = lax.optimization_barrier((far, near_queries[2]))
    far_queries = [swap(far, bits) for bits in near]
    spread = jnp.broadcast_to(lengths[:, None], (requests, STAT_LANES))
    near_parts = attend(spread, draft_mask, [mine, *near_queries], keys, spec, heads, latent)
    near_parts, far_queries = lax.optimization_barrier((near_parts, far_queries))
    far_parts = attend(spread, draft_mask, [far, *far_queries], keys, spec, heads, latent)
    near_parts, far_parts = lax.optimization_barrier((near_parts, far_parts))
    far_part = combine(
        [far_parts[0]]
        + [swap(far_parts[i + 1], near[i]) for i in (1, 0, *range(2, len(near)))],
        latent,
    )
    parts = [swap(far_part, far_bit), near_parts[0]]
    parts += [swap(part, bits) for part, bits in zip(near_parts[1:], near)]
    own, give = merge(parts, latent)
    outs = project(own, swap(give, 1), value_up, output_weight, spec, n)
    received = lax.all_to_all(outs, "ctx", 0, 0, tiled=True)
    return finish(received, requests)


def solution(mesh):
    return jax.shard_map(
        functools.partial(on_device, mesh.shape["ctx"]),
        mesh=mesh,
        in_specs=(
            P("grp", None, "ctx", None),
            P("grp", "ctx", None),
            P("grp"),
            P("grp", None),
            P("ctx", None, None),
            P("ctx", None),
        ),
        out_specs=P("grp", None, "ctx"),
        check_vma=False,
    )
```

```python
import functools
import math

import jax
import jax.numpy as jnp
from jax import lax
from jax.experimental import pallas as pl
from jax.experimental.pallas import tpu as pltpu
from jax.sharding import PartitionSpec as P

SOFTMAX_SCALE = 192.0 ** (-0.5)
LOG2_SCALE = SOFTMAX_SCALE * math.log2(math.e)
SCORE_FLOOR = -1e30
PEAK_FLOOR = -(2.0**96)
STAT_LANES = 128
STAT_ROWS = 8
MIB = 1024 * 1024
HINT = 20 * MIB


def split_low(x):
    high = x.astype(jnp.bfloat16).astype(jnp.float32)
    return high, (x - high).astype(jnp.bfloat16).astype(jnp.float32)


def select_kernel(own_ref, got_ref, out_ref):
    core = lax.rem(lax.axis_index("ctx"), 2)
    rows = out_ref.shape[0] // 2
    out_ref[:rows] = own_ref[...].reshape(rows, -1)
    out_ref[rows:] = got_ref[core].reshape(rows, -1)


def select(own, got):
    spec, heads, feature = own.shape
    return pl.pallas_call(
        select_kernel,
        out_shape=jax.ShapeDtypeStruct((2 * spec * heads, feature), own.dtype),
        compiler_params=pltpu.CompilerParams(vmem_limit_bytes=8 * MIB),
        cost_estimate=pl.CostEstimate(flops=0, bytes_accessed=HINT, transcendentals=0),
        name="select",
    )(own, got)


def attend_kernel(chunks, spec, heads, latent, lengths_ref, mask_ref, *refs):
    q_refs, key_refs, out_refs = refs[:chunks], refs[chunks : chunks + 2], refs[chunks + 2 :]
    block = key_refs[1].shape[1]
    width = min(block, 512)
    per_block = block // width
    steps = 2 * per_block
    me = lax.axis_index("ctx")
    bases = (me * block, (me + 1 - 2 * lax.rem(me, 2)) * block)
    queries = jnp.concatenate([ref[...] for ref in q_refs], axis=0)
    rows = queries.shape[0]
    row = lax.broadcasted_iota(jnp.int32, (rows, 1), 0)
    draft = lax.rem(lax.div(row, heads), spec)
    horizon = lengths_ref[pl.ds(lax.rem(me, 2), 1), :1] - spec + 1 + draft

    def keys(step, features):
        start = (step % per_block) * width
        if step < per_block:
            return key_refs[0][lax.rem(me, 2), :features, start : start + width]
        return key_refs[1][:features, start : start + width]

    def score(step):
        tile = jnp.dot(queries, keys(step, None), preferred_element_type=jnp.float32)
        start = bases[step // per_block] + (step % per_block) * width
        position = start + lax.broadcasted_iota(jnp.int32, (1, width), 1)
        return jnp.where(position < horizon, tile * LOG2_SCALE, SCORE_FLOOR)

    peak = jnp.full((rows, 1), PEAK_FLOOR, jnp.float32)
    denominator = jnp.zeros((rows, 1), jnp.float32)
    numerator = jnp.zeros((rows, latent), jnp.float32)
    half = steps // 2
    tiles = [score(step) for step in range(half)]
    for side in range(2):
        following = []
        higher = peak
        for tile in tiles:
            higher = jnp.maximum(higher, jnp.max(tile, axis=1, keepdims=True))
        if side == 1:
            higher = sum(split_low(higher))
        ratio = jnp.exp2(peak - higher)
        denominator *= ratio
        numerator *= ratio
        for i in range(half):
            if side == 0:
                following.append(score(half + i))
            weights = jnp.exp2(tiles[i] - higher)
            denominator += jnp.sum(weights, axis=1, keepdims=True)
            numerator += lax.dot_general(
                weights.astype(jnp.bfloat16),
                keys(side * half + i, latent),
                (((1,), (1,)), ((), ())),
                preferred_element_type=jnp.float32,
            )
        peak, tiles = higher, following
    mask = mask_ref[pl.ds(lax.rem(me, 2), 1), :].astype(jnp.float32)
    numerator *= sum(jnp.where(draft == j, mask[:, j : j + 1], 0.0) for j in range(spec))
    chunk = rows // chunks
    for i, out_ref in enumerate(out_refs):
        part = slice(i * chunk, (i + 1) * chunk)
        store_part(out_ref, latent, peak[part], denominator[part], numerator[part])


def attend(lengths, mask, query_chunks, keys, spec, heads, latent):
    chunks = len(query_chunks)
    chunk, feature = query_chunks[0].shape
    rows, positions = chunks * chunk, 2 * keys[1].shape[1]
    return pl.pallas_call(
        functools.partial(attend_kernel, chunks, spec, heads, latent),
        out_shape=[jax.ShapeDtypeStruct((chunk, latent + STAT_LANES), jnp.bfloat16)] * chunks,
        compiler_params=pltpu.CompilerParams(vmem_limit_bytes=12 * MIB),
        cost_estimate=pl.CostEstimate(
            flops=2 * rows * positions * (feature + latent),
            bytes_accessed=2 * positions * feature,
            transcendentals=rows * positions,
        ),
        name="attend",
    )(lengths, mask, *query_chunks, *keys)


def merged(in_refs, latent):
    peaks, denominators = [], []
    for ref in in_refs:
        rows = in_refs[-1].shape[0]
        if ref.shape[1] == latent:
            stats = ref[rows:, :STAT_LANES].astype(jnp.float32).T[:rows]
        else:
            stats = ref[:, latent:].astype(jnp.float32)
        peaks.append(stats[:, 0:1] + stats[:, 1:2])
        denominators.append(stats[:, 2:3] + stats[:, 3:4])
    largest = functools.reduce(jnp.maximum, peaks)
    upper, lower = 0.0, 0.0
    for ref, peak, denominator in zip(in_refs, peaks, denominators):
        factor = jnp.exp2(peak - largest)
        upper += factor * ref[: peak.shape[0], :latent].astype(jnp.float32)
        lower += factor * denominator
    return largest, lower, upper


def store_part(ref, latent, peak, denominator, numerator):
    peak_high, peak_low = split_low(peak)
    denom_high, denom_low = split_low(denominator)
    lane = lax.broadcasted_iota(jnp.int32, (ref.shape[0], STAT_LANES), 1)
    stats = jnp.where(lane == 0, peak_high, jnp.where(lane == 1, peak_low, 0.0))
    stats = jnp.where(lane == 2, denom_high, jnp.where(lane == 3, denom_low, stats))
    ref[:, :latent] = numerator.astype(jnp.bfloat16)
    ref[:, latent:] = stats.astype(jnp.bfloat16)


def store_packed(ref, latent, peak, denominator, numerator):
    rows = numerator.shape[0]
    peak_high, peak_low = split_low(peak)
    denom_high, denom_low = split_low(denominator)
    lane = lax.broadcasted_iota(jnp.int32, (rows, STAT_LANES), 1)
    stats = jnp.where(lane == 0, peak_high, jnp.where(lane == 1, peak_low, 0.0))
    stats = jnp.where(lane == 2, denom_high, jnp.where(lane == 3, denom_low, stats))
    blank = jnp.zeros((STAT_LANES - rows, STAT_LANES), jnp.float32)
    stats = jnp.concatenate([stats, blank], axis=0).T[:STAT_ROWS]
    ref[:rows] = numerator.astype(jnp.bfloat16)
    ref[rows:] = jnp.zeros((STAT_ROWS, latent), jnp.bfloat16)
    ref[rows:, :STAT_LANES] = stats.astype(jnp.bfloat16)


def combine_kernel(parts, latent, *refs):
    store_packed(refs[parts], latent, *merged(refs[:parts], latent))


def combine(parts, latent):
    return pl.pallas_call(
        functools.partial(combine_kernel, len(parts), latent),
        out_shape=jax.ShapeDtypeStruct((parts[0].shape[0] + STAT_ROWS, latent), jnp.bfloat16),
        compiler_params=pltpu.CompilerParams(vmem_limit_bytes=8 * MIB),
        name="combine",
    )(*parts)


def merge_kernel(parts, latent, *refs):
    _, lower, upper = merged(refs[:parts], latent)
    own_ref, give_ref = refs[parts:]
    attended = (upper / lower).astype(jnp.bfloat16)
    half = attended.shape[0] // 2
    own_ref[...] = attended[:half]
    give_ref[...] = attended[half:]


def merge(parts, latent):
    rows = parts[-1].shape[0]
    return pl.pallas_call(
        functools.partial(merge_kernel, len(parts), latent),
        out_shape=[jax.ShapeDtypeStruct((rows // 2, latent), jnp.bfloat16)] * 2,
        compiler_params=pltpu.CompilerParams(vmem_limit_bytes=8 * MIB),
        name="merge",
    )(*parts)


def project_kernel(heads, group, own_ref, got_ref, up_ref, weight_ref, out_ref):
    core = lax.rem(lax.axis_index("ctx"), 2)
    own, got = own_ref[...], got_ref[...]
    first = jnp.where(core == 0, own, got)
    second = jnp.where(core == 0, got, own)
    attended = jnp.concatenate([first, second], axis=0)
    rows = attended.shape[0]
    head = lax.rem(lax.broadcasted_iota(jnp.int32, (rows, 1), 0), heads)
    values = []
    for h in range(heads):
        tile = jnp.dot(attended, up_ref[h], preferred_element_type=jnp.float32)
        tile = jnp.where(head == h, tile, 0.0)
        tile = jnp.sum(tile.reshape(rows // heads, heads, tile.shape[1]), axis=1)
        values.append(tile.astype(jnp.bfloat16))
    values = jnp.concatenate(values, axis=1)
    owners, _, columns = out_ref.shape
    for i in range(0, owners, group):
        part = weight_ref[:, i * columns : (i + group) * columns]
        tile = jnp.dot(values, part, preferred_element_type=jnp.float32)
        for j in range(group):
            piece = tile[:, j * columns : (j + 1) * columns]
            out_ref[i + j] = piece.astype(out_ref.dtype)


def project(own, got, value_up, weight, spec, owners):
    heads = own.shape[0] // spec
    columns = weight.shape[1] // owners
    group = next(g for g in (8, 4, 2, 1, 16, owners) if (g * columns) % 128 == 0)
    return pl.pallas_call(
        functools.partial(project_kernel, heads, group),
        out_shape=jax.ShapeDtypeStruct((owners, 2 * spec, columns), jnp.bfloat16),
        in_specs=[pl.BlockSpec(memory_space=pltpu.VMEM)] * 4,
        out_specs=pl.BlockSpec(memory_space=pltpu.VMEM),
        compiler_params=pltpu.CompilerParams(vmem_limit_bytes=12 * MIB),
        name="project",
    )(own, got, value_up, weight)


def finish_kernel(in_ref, out_ref):
    total = jnp.sum(in_ref[...].astype(jnp.float32), axis=0)
    spec = out_ref.shape[1]
    for r in range(out_ref.shape[0]):
        out_ref[r] = total[r * spec : (r + 1) * spec].astype(out_ref.dtype)


def finish(parts, requests):
    _, rows, columns = parts.shape
    return pl.pallas_call(
        finish_kernel,
        out_shape=jax.ShapeDtypeStruct((requests, rows // requests, columns), jnp.bfloat16),
        compiler_params=pltpu.CompilerParams(vmem_limit_bytes=8 * MIB),
        name="finish",
    )(parts)


def on_device(n, queries, latent_cache, lengths, draft_mask, value_up, output_weight):
    requests, spec, heads, feature = queries.shape
    latent = value_up.shape[1]
    core = lax.rem(lax.axis_index("ctx"), 2)

    def swap(x, bits):
        return lax.ppermute(x, "ctx", [(i, i ^ bits) for i in range(n)])

    chunk = requests * spec * heads
    got = swap(queries, 1)
    own_queries = lax.dynamic_index_in_dim(queries, core, 0, keepdims=False)
    own_queries, got = lax.optimization_barrier((own_queries, got))
    mine = select(own_queries, got)
    own_keys = jnp.swapaxes(latent_cache, 1, 2)
    got_keys = swap(lax.optimization_barrier((own_keys, got))[0], 1)

    far_bit = n // 2
    near = [2 * k for k in range(1, n // 4)][::-1]
    far = swap(mine, far_bit)
    near_queries = [swap(mine, bits) for bits in near]

    keys = [own_keys, lax.dynamic_index_in_dim(got_keys, core, 0, keepdims=False)]
    far, near_queries[2] = lax.optimization_barrier((far, near_queries[2]))
    far_queries = [swap(far, bits) for bits in near]
    spread = jnp.broadcast_to(lengths[:, None], (requests, STAT_LANES))
    near_parts = attend(spread, draft_mask, [mine, *near_queries], keys, spec, heads, latent)
    near_parts, far_queries = lax.optimization_barrier((near_parts, far_queries))
    far_parts = attend(spread, draft_mask, [far, *far_queries], keys, spec, heads, latent)
    near_parts, far_parts = lax.optimization_barrier((near_parts, far_parts))
    far_part = combine(
        [far_parts[0]]
        + [swap(far_parts[i + 1], near[i]) for i in (1, 0, *range(2, len(near)))],
        latent,
    )
    parts = [swap(far_part, far_bit), near_parts[0]]
    parts += [swap(part, bits) for part, bits in zip(near_parts[1:], near)]
    own, give = merge(parts, latent)
    outs = project(own, swap(give, 1), value_up, output_weight, spec, n)
    received = lax.all_to_all(outs, "ctx", 0, 0, tiled=True)
    return finish(received, requests)


def solution(mesh):
    return jax.shard_map(
        functools.partial(on_device, mesh.shape["ctx"]),
        mesh=mesh,
        in_specs=(
            P("grp", None, "ctx", None),
            P("grp", "ctx", None),
            P("grp"),
            P("grp", None),
            P("ctx", None, None),
            P("ctx", None),
        ),
        out_specs=P("grp", None, "ctx"),
        check_vma=False,
    )
```

```python
import functools
import math

import jax
import jax.numpy as jnp
from jax import lax
from jax.experimental import pallas as pl
from jax.experimental.pallas import tpu as pltpu
from jax.sharding import PartitionSpec as P

SOFTMAX_SCALE = 192.0 ** (-0.5)
LOG2_SCALE = SOFTMAX_SCALE * math.log2(math.e)
SCORE_FLOOR = -1e30
STAT_LANES = 128
MIB = 1024 * 1024
HINT = 20 * MIB


def split_low(x):
    high = x.astype(jnp.bfloat16).astype(jnp.float32)
    return high, (x - high).astype(jnp.bfloat16).astype(jnp.float32)


def select_kernel(own_ref, got_ref, out_ref):
    core = lax.rem(lax.axis_index("ctx"), 2)
    rows = out_ref.shape[0] // 2
    out_ref[:rows] = own_ref[...].reshape(rows, -1)
    out_ref[rows:] = got_ref[core].reshape(rows, -1)


def select(own, got):
    spec, heads, feature = own.shape
    return pl.pallas_call(
        select_kernel,
        out_shape=jax.ShapeDtypeStruct((2 * spec * heads, feature), own.dtype),
        compiler_params=pltpu.CompilerParams(vmem_limit_bytes=8 * MIB),
        cost_estimate=pl.CostEstimate(flops=0, bytes_accessed=HINT, transcendentals=0),
        name="select",
    )(own, got)


def attend_kernel(chunks, spec, heads, latent, lengths_ref, mask_ref, *refs):
    q_refs, key_refs, out_refs = refs[:chunks], refs[chunks : chunks + 2], refs[chunks + 2 :]
    block = key_refs[1].shape[1]
    width = min(block, 512)
    per_block = block // width
    steps = 2 * per_block
    me = lax.axis_index("ctx")
    bases = (me * block, (me + 1 - 2 * lax.rem(me, 2)) * block)
    queries = jnp.concatenate([ref[...] for ref in q_refs], axis=0)
    rows = queries.shape[0]
    row = lax.broadcasted_iota(jnp.int32, (rows, 1), 0)
    draft = lax.rem(lax.div(row, heads), spec)
    horizon = lengths_ref[pl.ds(lax.rem(me, 2), 1), :1] - spec + 1 + draft

    def keys(step, features):
        start = (step % per_block) * width
        if step < per_block:
            return key_refs[0][lax.rem(me, 2), :features, start : start + width]
        return key_refs[1][:features, start : start + width]

    def score(step):
        tile = jnp.dot(queries, keys(step, None), preferred_element_type=jnp.float32)
        start = bases[step // per_block] + (step % per_block) * width
        position = start + lax.broadcasted_iota(jnp.int32, (1, width), 1)
        return jnp.where(position < horizon, tile * LOG2_SCALE, SCORE_FLOOR)

    peak = jnp.full((rows, 1), 0.1 * SCORE_FLOOR, jnp.float32)
    denominator = jnp.zeros((rows, 1), jnp.float32)
    numerator = jnp.zeros((rows, latent), jnp.float32)
    tile = score(0)
    for step in range(steps):
        following = score(step + 1) if step + 1 < steps else None
        higher = jnp.maximum(peak, jnp.max(tile, axis=1, keepdims=True))
        if step == steps - 1:
            higher = sum(split_low(higher))
        weights = jnp.exp2(tile - higher)
        ratio = jnp.exp2(peak - higher)
        denominator = denominator * ratio + jnp.sum(weights, axis=1, keepdims=True)
        numerator = numerator * ratio + lax.dot_general(
            weights.astype(jnp.bfloat16),
            keys(step, latent),
            (((1,), (1,)), ((), ())),
            preferred_element_type=jnp.float32,
        )
        peak, tile = higher, following
    mask = mask_ref[pl.ds(lax.rem(me, 2), 1), :].astype(jnp.float32)
    numerator *= sum(jnp.where(draft == j, mask[:, j : j + 1], 0.0) for j in range(spec))
    chunk = rows // chunks
    for i, out_ref in enumerate(out_refs):
        part = slice(i * chunk, (i + 1) * chunk)
        store_part(out_ref, latent, peak[part], denominator[part], numerator[part])


def attend(lengths, mask, query_chunks, keys, spec, heads, latent):
    chunks = len(query_chunks)
    chunk, feature = query_chunks[0].shape
    rows, positions = chunks * chunk, 2 * keys[1].shape[1]
    return pl.pallas_call(
        functools.partial(attend_kernel, chunks, spec, heads, latent),
        out_shape=[jax.ShapeDtypeStruct((chunk, latent + STAT_LANES), jnp.bfloat16)] * chunks,
        compiler_params=pltpu.CompilerParams(vmem_limit_bytes=12 * MIB),
        cost_estimate=pl.CostEstimate(
            flops=2 * rows * positions * (feature + latent),
            bytes_accessed=2 * positions * feature,
            transcendentals=rows * positions,
        ),
        name="attend",
    )(lengths, mask, *query_chunks, *keys)


def merged(in_refs, latent):
    peaks, denominators = [], []
    for ref in in_refs:
        stats = ref[:, latent:].astype(jnp.float32)
        peaks.append(stats[:, 0:1] + stats[:, 1:2])
        denominators.append(stats[:, 2:3] + stats[:, 3:4])
    largest = functools.reduce(jnp.maximum, peaks)
    upper, lower = 0.0, 0.0
    for ref, peak, denominator in zip(in_refs, peaks, denominators):
        factor = jnp.exp2(peak - largest)
        upper += factor * ref[:, :latent].astype(jnp.float32)
        lower += factor * denominator
    return largest, lower, upper


def store_part(ref, latent, peak, denominator, numerator):
    peak_high, peak_low = split_low(peak)
    denom_high, denom_low = split_low(denominator)
    lane = lax.broadcasted_iota(jnp.int32, (ref.shape[0], STAT_LANES), 1)
    stats = jnp.where(lane == 0, peak_high, jnp.where(lane == 1, peak_low, 0.0))
    stats = jnp.where(lane == 2, denom_high, jnp.where(lane == 3, denom_low, stats))
    ref[:, :latent] = numerator.astype(jnp.bfloat16)
    ref[:, latent:] = stats.astype(jnp.bfloat16)


def combine_kernel(parts, latent, *refs):
    store_part(refs[parts], latent, *merged(refs[:parts], latent))


def combine(parts, latent):
    return pl.pallas_call(
        functools.partial(combine_kernel, len(parts), latent),
        out_shape=jax.ShapeDtypeStruct(parts[0].shape, jnp.bfloat16),
        compiler_params=pltpu.CompilerParams(vmem_limit_bytes=8 * MIB),
        name="combine",
    )(*parts)


def merge_kernel(parts, latent, *refs):
    _, lower, upper = merged(refs[:parts], latent)
    own_ref, give_ref = refs[parts:]
    attended = (upper / lower).astype(jnp.bfloat16)
    half = attended.shape[0] // 2
    own_ref[...] = attended[:half]
    give_ref[...] = attended[half:]


def merge(parts, latent):
    rows = parts[0].shape[0]
    return pl.pallas_call(
        functools.partial(merge_kernel, len(parts), latent),
        out_shape=[jax.ShapeDtypeStruct((rows // 2, latent), jnp.bfloat16)] * 2,
        compiler_params=pltpu.CompilerParams(vmem_limit_bytes=8 * MIB),
        name="merge",
    )(*parts)


def project_kernel(heads, group, own_ref, got_ref, up_ref, weight_ref, out_ref):
    core = lax.rem(lax.axis_index("ctx"), 2)
    own, got = own_ref[...], got_ref[...]
    first = jnp.where(core == 0, own, got)
    second = jnp.where(core == 0, got, own)
    attended = jnp.concatenate([first, second], axis=0)
    rows = attended.shape[0]
    head = lax.rem(lax.broadcasted_iota(jnp.int32, (rows, 1), 0), heads)
    values = []
    for h in range(heads):
        tile = jnp.dot(attended, up_ref[h], preferred_element_type=jnp.float32)
        tile = jnp.where(head == h, tile, 0.0)
        tile = jnp.sum(tile.reshape(rows // heads, heads, tile.shape[1]), axis=1)
        values.append(tile.astype(jnp.bfloat16))
    values = jnp.concatenate(values, axis=1)
    owners, _, columns = out_ref.shape
    for i in range(0, owners, group):
        part = weight_ref[:, i * columns : (i + group) * columns]
        tile = jnp.dot(values, part, preferred_element_type=jnp.float32)
        for j in range(group):
            piece = tile[:, j * columns : (j + 1) * columns]
            out_ref[i + j] = piece.astype(out_ref.dtype)


def project(own, got, value_up, weight, spec, owners):
    heads = own.shape[0] // spec
    columns = weight.shape[1] // owners
    group = next(g for g in (2, 1, 4, 8, 16, owners) if (g * columns) % 128 == 0)
    return pl.pallas_call(
        functools.partial(project_kernel, heads, group),
        out_shape=jax.ShapeDtypeStruct((owners, 2 * spec, columns), jnp.bfloat16),
        in_specs=[pl.BlockSpec(memory_space=pltpu.VMEM)] * 4,
        out_specs=pl.BlockSpec(memory_space=pltpu.VMEM),
        compiler_params=pltpu.CompilerParams(vmem_limit_bytes=12 * MIB),
        name="project",
    )(own, got, value_up, weight)


def on_device(n, queries, latent_cache, lengths, draft_mask, value_up, output_weight):
    requests, spec, heads, feature = queries.shape
    latent = value_up.shape[1]
    core = lax.rem(lax.axis_index("ctx"), 2)

    def swap(x, bits):
        return lax.ppermute(x, "ctx", [(i, i ^ bits) for i in range(n)])

    chunk = requests * spec * heads
    got = swap(queries, 1)
    own_queries = lax.dynamic_index_in_dim(queries, core, 0, keepdims=False)
    own_queries, got = lax.optimization_barrier((own_queries, got))
    mine = select(own_queries, got)
    own_keys = jnp.swapaxes(latent_cache, 1, 2)
    got_keys = swap(lax.optimization_barrier((own_keys, got))[0], 1)

    far_bit = n // 2
    near = [2 * k for k in range(1, n // 4)][::-1]
    far = swap(mine, far_bit)
    near_queries = [swap(mine, bits) for bits in near]

    keys = [own_keys, lax.dynamic_index_in_dim(got_keys, core, 0, keepdims=False)]
    far, near_queries[2] = lax.optimization_barrier((far, near_queries[2]))
    far_queries = [swap(far, bits) for bits in near]
    spread = jnp.broadcast_to(lengths[:, None], (requests, STAT_LANES))
    near_parts = attend(spread, draft_mask, [mine, *near_queries], keys, spec, heads, latent)
    near_parts, far_queries = lax.optimization_barrier((near_parts, far_queries))
    far_parts = attend(spread, draft_mask, [far, *far_queries], keys, spec, heads, latent)
    near_parts, far_parts = lax.optimization_barrier((near_parts, far_parts))
    far_part = combine(
        [far_parts[0]]
        + [swap(far_parts[i + 1], near[i]) for i in (1, 0, *range(2, len(near)))],
        latent,
    )
    parts = [swap(far_part, far_bit), near_parts[0]]
    parts += [swap(part, bits) for part, bits in zip(near_parts[1:], near)]
    own, give = merge(parts, latent)
    outs = project(own, swap(give, 1), value_up, output_weight, spec, n)
    received = lax.all_to_all(outs, "ctx", 0, 0, tiled=True)
    total = jnp.sum(received.astype(jnp.float32), axis=0).astype(jnp.bfloat16)
    return total.reshape(requests, spec, -1)


def solution(mesh):
    return jax.shard_map(
        functools.partial(on_device, mesh.shape["ctx"]),
        mesh=mesh,
        in_specs=(
            P("grp", None, "ctx", None),
            P("grp", "ctx", None),
            P("grp"),
            P("grp", None),
            P("ctx", None, None),
            P("ctx", None),
        ),
        out_specs=P("grp", None, "ctx"),
        check_vma=False,
    )
```
